128 devices in a mesh: pool: 4 (over x_lo, core), dev: 32 (over x_hi, y, z).
Axes of the slice: x: 4 (x_hi: 2, x_lo: 2; x = x_hi * 2 + x_lo), y: 4, z: 4, core: 2. Of those that a mesh axis runs over, the one named last changes fastest.
Arguments:
- query: bfloat16 [512, 3072], P(('pool', 'dev')), may hold values from -90 to 90
- new_key: bfloat16 [512, 512], P(('pool', 'dev')), may hold values from -4 to 4
- new_value: bfloat16 [512, 512], P(('pool', 'dev')), may hold values from -6 to 6
- key_cache: bfloat16 [512, 512, 512], P(('pool', 'dev')), may hold values from -3 to 3
- value_cache: bfloat16 [512, 512, 512], P(('pool', 'dev')), may hold values from -6 to 6
- lengths: int32 [512], P(('pool', 'dev')), may hold values from 64 to 512, as said below
- hidden_in: bfloat16 [512, 6144], P('pool', 'dev'), may hold values from -6 to 6
- w_out: bfloat16 [3072, 6144], P(None, 'dev'), may hold values from -0.5 to 0.5
- expert_ids: int32 [512, 2], P('pool'), may hold values from 0 to 7, all different within a row; in each aligned block of 128 rows (0 to 127, 128 to 255, ...) at most 80 rows name the same one
- gate_weights: float32 [512, 2], P('pool'), may hold values from 0.2 to 1
- w_gate: bfloat16 [8, 6144, 8192], P('pool', None, 'dev'), may hold values from -0.078125 to 0.078125
- w_up: bfloat16 [8, 6144, 8192], P('pool', None, 'dev'), may hold values from -0.078125 to 0.078125
- w_down: bfloat16 [8, 8192, 6144], P('pool', 'dev'), may hold values from -0.125 to 0.125
Outputs:
- mixed: bfloat16 [512, 6144], P('pool', 'dev')
The draws below stay inside these ranges and needn't reach their ends.
Inputs may be any that keep to these rules, and one draw needn't show every extreme that they name: `expert_ids`: every row names 2 different experts; among the rows of one micro-batch (aligned blocks of 128 rows) no expert is named by more than 80 rows, a bound that some block reaches. `lengths`: some row has all 512 positions in use.
All inputs are finite; a program needn't handle non-finite values.
Results may differ from the reference program's by a relative error of at most 0.011.
Values may be sent and summed in bfloat16 or wider, within the bound.
A program may use at most 192 MiB of HBM per device.

```python
import math
import jax
import jax.numpy as jnp
import numpy as np
from jax import lax

D = 6144
FFW = 8192
EXPERTS = 8
TOP = 2
HEADS = 24
KV_HEADS = 4
HEAD_DIM = 128
CTX = 512
ROWS_GRP = 128
ROWS = 512
CAP = 80
N_POOL = 4


def cache_keys(key):
    raw = jax.random.normal(jax.random.fold_in(key, 11), (ROWS, CTX, KV_HEADS * HEAD_DIM), jnp.float32)
    return jnp.clip(raw, -3.0, 3.0)


def draw_key_cache(key, part):
    shared = cache_keys(key)
    return shared.astype(jnp.bfloat16)


def draw_query(key, part):
    key = jax.random.fold_in(key, 2)
    values = jnp.clip(jax.random.normal(key, (ROWS, HEADS * HEAD_DIM), jnp.float32), -4.0, 4.0)
    return values.astype(jnp.bfloat16)


def draw_lengths(key, part):
    key = jax.random.fold_in(key, 7)
    values = jax.random.randint(key, (ROWS,), CTX // 8, CTX + 1)
    return jnp.where(jnp.arange(ROWS) == 0, CTX, values).astype(jnp.int32)


def with_spikes(drawn, own_key, source, target, shards_of, factor):
    owner, partner = [(jnp.arange(drawn.shape[axis_at]) // (drawn.shape[axis_at] // shards_of)).reshape([-1 if axis == axis_at else 1 for axis in range(drawn.ndim)]) for axis_at in (source, target)]
    chosen = jax.random.permutation(own_key, shards_of)[partner]
    strong = (owner == chosen) | (owner == (partner + shards_of // 2) % shards_of)
    return jnp.where(strong, factor * drawn, drawn)


def block_scale(rng, shape, pieces, smallest, largest):
    def one(position, blocks):
        heights = jax.random.uniform(jax.random.fold_in(jax.random.fold_in(rng, 6), position), (blocks,), jnp.float32, smallest / len(pieces), largest / len(pieces))
        return jnp.repeat(jnp.exp(heights), shape[position] // blocks).reshape((-1,) + (1,) * (len(shape) - position - 1))

    loudness = one(*pieces[0])
    for cut in pieces[1:]:
        loudness = loudness * one(*cut)
    return loudness


def routed_block(key, own, number, rows, number_of, top, most, slope):
    sequence = jax.random.permutation(key, number_of)
    heavy_load, ordinary = shares(number_of, rows * top, most, slope, True), shares(number_of, rows * top, most, slope, False)
    places = jnp.arange(number_of)

    def named(tallies, turn):
        used = int((tallies > 0).sum())
        fixed = max(1, used // 4)
        passed = fixed + (places - fixed + turn * (used - fixed)) % max(1, number_of - fixed)
        return jnp.zeros((number_of,), jnp.int32).at[sequence[jnp.where(places < fixed, places, passed)]].set(jnp.asarray(tallies, jnp.int32))

    tallies = jnp.where(number % 4 == 0, named(heavy_load, number // 4), named(ordinary, number - number // 4 - 1))
    mixed = jax.random.permutation(jax.random.fold_in(own, 3), number_of)
    giver, receiver = mixed[0:number_of // 2 * 2:2], mixed[1:number_of // 2 * 2:2]
    margin = jnp.minimum(tallies[giver] - 1, most - tallies[receiver]) // 2
    margin = jnp.where((giver == sequence[0]) | (receiver == sequence[0]) | (tallies[receiver] == 0), 0, jnp.maximum(margin, 0))
    passed = jax.random.randint(jax.random.fold_in(own, 4), (number_of // 2,), 0, 1 << 20) % (margin + 1)
    tallies = tallies.at[giver].add(-passed).at[receiver].add(passed)
    items = jnp.searchsorted(jnp.cumsum(tallies), jnp.arange(rows * top), side="right").astype(jnp.int32)
    table = items.reshape(top, rows).T
    table = table[jax.random.permutation(jax.random.fold_in(own, 1), rows)]
    turn = jax.random.randint(jax.random.fold_in(own, 2), (rows, 1), 0, top)
    return jnp.take_along_axis(table, (jnp.arange(top)[None, :] + turn) % top, axis=1)


def shares(number_of, total, most, slope, full):
    portions = [(1 << 20) // math.isqrt(rank ** slope) + 1 for rank in range(1, number_of + 1)]
    largest = most if full else min(most, max(-(-total // number_of), total * portions[0] // sum(portions)))
    least = 1 if total - largest >= number_of - 1 else 0
    holding, surplus = [largest] + [least] * (number_of - 1), total - largest - least * (number_of - 1)
    while surplus > 0:
        free = [i for i in range(1, number_of) if holding[i] < largest] or [i for i in range(1, number_of) if holding[i] < most]
        whole, budget = sum([portions[i] for i in free]), surplus
        for i in free:
            more = min(most - holding[i], max(1, budget * portions[i] // whole), surplus)
            holding[i] = holding[i] + more
            surplus = surplus - more
    return np.array(holding)


def centred(own_key, dims, spread, bound, cuts=(), held_as=jnp.bfloat16):
    entries = jax.random.normal(own_key, dims, jnp.float32) * spread
    if len(cuts) > 0:
        entries = block_scale(own_key, dims, cuts, -0.22, 0.18) * entries
    return jnp.clip(entries, min=-bound, max=bound).astype(held_as)


def heavy_noise(key, dims, deviation, bound, split, heavy, held_as=jnp.bfloat16):
    array = deviation * jax.random.normal(key, dims, jnp.float32)
    if split:
        array = array * block_scale(key, dims, split, -0.22, 0.18)
    return jnp.clip(with_spikes(array, jax.random.fold_in(key, 3), *heavy), -bound, bound).astype(held_as)


def setup_inputs(seed: int = 0) -> dict:
    splits = jax.random.split(jax.random.key(seed), 14)
    query = draw_query(jax.random.fold_in(splits[13], 71), 0)
    new_key = centred(splits[1], (ROWS, KV_HEADS * HEAD_DIM), 1.0, 4.0, ((0, 128),))
    new_value = centred(splits[2], (ROWS, KV_HEADS * HEAD_DIM), 1.0, 6.0, ((0, 128),))
    key_cache = draw_key_cache(jax.random.fold_in(splits[13], 71), 0)
    value_cache = centred(splits[4], (ROWS, CTX, KV_HEADS * HEAD_DIM), 1.0, 6.0, ((0, 128),))
    lengths = draw_lengths(jax.random.fold_in(splits[13], 71), 0)
    hidden_in = centred(splits[6], (ROWS, D), 1.0, 6.0, ((0, 4), (1, 32)))
    w_out = centred(splits[7], (HEADS * HEAD_DIM, D), HEAD_DIM ** -0.5, 0.5, ((1, 32),))
    expert_ids_keys = jax.random.split(jax.random.fold_in(splits[8], 1), ROWS // ROWS_GRP)
    expert_ids_turns = jax.random.permutation(jax.random.fold_in(splits[8], 3), ROWS // ROWS_GRP)
    expert_ids = jax.vmap(lambda own, number: routed_block(jax.random.fold_in(splits[8], 2), own, number, ROWS_GRP, EXPERTS, TOP, CAP, 2))(expert_ids_keys, expert_ids_turns).reshape((ROWS, TOP))
    gate_weights = jnp.clip(0.2 + 0.8 * jax.random.uniform(splits[9], (ROWS, TOP), jnp.float32) ** block_scale(splits[9], (ROWS, TOP), ((0, 4),), -0.2, 0.2), 0.2, 1.0)
    w_gate = centred(splits[10], (EXPERTS, D, FFW), D ** -0.5, 0.078125, ((0, 4), (2, 32)))
    w_up = centred(splits[11], (EXPERTS, D, FFW), D ** -0.5, 0.078125, ((0, 4), (2, 32)))
    w_down = heavy_noise(splits[12], (EXPERTS, FFW, D), FFW ** -0.5, 0.125, ((0, 4), (1, 32)), (1, 2, 32, 2.75))
    return {"query": query, "new_key": new_key, "new_value": new_value, "key_cache": key_cache, "value_cache": value_cache, "lengths": lengths, "hidden_in": hidden_in, "w_out": w_out, "expert_ids": expert_ids, "gate_weights": gate_weights, "w_gate": w_gate, "w_up": w_up, "w_down": w_down}


floor_value = -1.0e30


def attention(query, new_key, new_value, key_cache, value_cache, lengths):
    row_count = query.shape[0]
    group_size = HEADS // KV_HEADS
    score_scale = HEAD_DIM ** -0.5
    highest = lax.Precision.HIGHEST
    queries = query.astype(jnp.float32).reshape(row_count, KV_HEADS, group_size, HEAD_DIM)
    cached_keys = key_cache.astype(jnp.float32).reshape(row_count, CTX, KV_HEADS, HEAD_DIM)
    cached_values = value_cache.astype(jnp.float32).reshape(row_count, CTX, KV_HEADS, HEAD_DIM)
    scores = jnp.einsum("rkgd,rtkd->rkgt", queries, cached_keys, precision=highest) * score_scale
    usable = (jnp.arange(CTX)[None, :] < lengths[:, None])[:, None, None, :]
    row_max = jnp.max(jnp.where(usable, scores, floor_value), axis=-1)
    weights = jnp.where(usable, jnp.exp(scores - row_max[..., None]), 0.0)
    weight_total = jnp.sum(weights, axis=-1)
    rounded = lax.optimization_barrier(weights.astype(jnp.bfloat16)).astype(jnp.float32)
    cache_sum = jnp.einsum("rkgt,rtkd->rkgd", rounded, cached_values, precision=highest)
    fresh_keys = new_key.astype(jnp.float32).reshape(row_count, KV_HEADS, HEAD_DIM)
    fresh_score = jnp.einsum("rkgd,rkd->rkg", queries, fresh_keys, precision=highest) * score_scale
    final_max = jnp.maximum(row_max, fresh_score)
    cache_factor = jnp.exp(row_max - final_max)
    fresh_factor = jnp.exp(fresh_score - final_max)
    fresh_values = new_value.astype(jnp.float32).reshape(row_count, KV_HEADS, 1, HEAD_DIM)
    numerator = cache_sum * cache_factor[..., None] + fresh_factor[..., None] * fresh_values
    attended = numerator / (weight_total * cache_factor + fresh_factor)[..., None]
    return attended.reshape(row_count, HEADS * HEAD_DIM).astype(jnp.bfloat16)


def experts(middle, expert_ids, gate_weights, w_gate, w_up, w_down):
    slot_count = N_POOL * CAP
    picked = expert_ids[:, :, None] == jnp.arange(EXPERTS)[None, None, :]
    routed = jnp.any(picked, axis=1)
    route = jnp.sum(jnp.where(picked, gate_weights[:, :, None], 0.0), axis=1)
    routed_int = routed.astype(jnp.int32)
    earlier = jnp.cumsum(routed_int, axis=0) - routed_int
    placed = routed[:, :, None] & (earlier[:, :, None] == jnp.arange(slot_count)[None, None, :])
    table = placed.astype(jnp.float32)
    gathered = jnp.einsum("res,rd->esd", table, middle.astype(jnp.float32), precision=lax.Precision.HIGHEST).astype(jnp.bfloat16)

    def one_expert(items):
        rows_in, gate_mat, up_mat, down_mat = items
        gate = jnp.dot(rows_in, gate_mat, preferred_element_type=jnp.float32)
        upward = jnp.dot(rows_in, up_mat, preferred_element_type=jnp.float32)
        hidden = (jax.nn.silu(gate) * upward).astype(jnp.bfloat16)
        return jnp.dot(hidden, down_mat, preferred_element_type=jnp.float32)

    outputs = lax.map(one_expert, (gathered, w_gate, w_up, w_down))
    weighted = table * route[:, :, None]
    return jnp.einsum("res,esd->rd", weighted, outputs, precision=lax.Precision.HIGHEST)


def reference(query, new_key, new_value, key_cache, value_cache, lengths, hidden_in, w_out, expert_ids, gate_weights, w_gate, w_up, w_down):
    attended = attention(query, new_key, new_value, key_cache, value_cache, lengths)
    projected = jnp.dot(attended, w_out, preferred_element_type=jnp.float32)
    middle = (hidden_in.astype(jnp.float32) + projected).astype(jnp.bfloat16)
    mixture = experts(middle, expert_ids, gate_weights, w_gate, w_up, w_down)
    return (middle.astype(jnp.float32) + mixture).astype(jnp.bfloat16)
```

```python
import jax
import jax.numpy as jnp
from jax import lax
from jax.experimental import pallas as pl
from jax.experimental.pallas import tpu as pltpu
from jax.sharding import PartitionSpec as P

EXPERTS = 8
HEADS = 24
KV_HEADS = 4
HEAD_DIM = 128
WIDTH = 6144
UNITS = 256

MESH = pl.DeviceIdType.MESH
floor_value = -1e30

GATHER_ORDER = ("zyx", "yxz", "xzy")
REDUCE_ORDER = ("xyz", "zxy", "yzx")


def layer_kernel(
    att_ref, ids_ref, weight_ref, hidden_ref, wout_ref, wg_hbm, wu_hbm, wd_hbm,
    out_ref,
    wcat, wd, at, g, route, s_mine, s_sib, from_sib, ring1, ring2, ring3, acc, hs_mine, hs_sib, mid, fin,
    lsem, ssem, rsem,
):
    f32, bf16 = jnp.float32, jnp.bfloat16
    pool, dev = lax.axis_index("pool"), lax.axis_index("dev")
    xl, c = pool // 2, pool % 2
    xh, y, z = dev // 16, (dev // 4) % 4, dev % 4
    x = 2 * xh + xl
    odd = (z % 2) == 1
    where_at = {"x": x, "y": y, "z": z}

    def ident(x_, y_, z_, c_):
        return ((x_ % 2) * 2 + c_, (x_ // 2) * 16 + y_ * 4 + z_)

    def near(axis, step):
        p = dict(where_at)
        p[axis] = (p[axis] + step + 4) % 4
        return ident(p["x"], p["y"], p["z"], c)

    sibling = ident(x, y, z, 1 - c)
    opposite = ident((x + 2) % 4, y, z, c)
    beside = x + 1 - 2 * xl
    beside_same = ident(beside, y, z, c)
    beside_other = ident(beside, y, z, 1 - c)

    local = []
    for e in range(2):
        for half in range(2):
            rows = pl.ds(half * (WIDTH // 2), WIDTH // 2)
            local.append(pltpu.make_async_copy(
                wg_hbm.at[e, rows], wcat.at[rows, pl.ds(e * 512, UNITS)], lsem.at[len(local)]))
            local.append(pltpu.make_async_copy(
                wu_hbm.at[e, rows], wcat.at[rows, pl.ds(e * 512 + UNITS, UNITS)], lsem.at[len(local)]))
    n_up = len(local)
    for e in range(2):
        local.append(pltpu.make_async_copy(wd_hbm.at[e], wd.at[pl.ds(e * UNITS, UNITS)], lsem.at[len(local)]))
    for cp in local:
        cp.start()

    barrier = pltpu.get_barrier_semaphore()
    greeted = [near(a, d) for a in "xyz" for d in (1, -1)] + [sibling, opposite, beside_other]
    for who in greeted:
        pl.semaphore_signal(barrier, inc=1, device_id=who, device_id_type=MESH)

    at[0, xh, y, z] = att_ref[0:48]
    at[1, xh, y, z] = att_ref[48:96]
    lane = lax.broadcasted_iota(jnp.int32, (128, 128), 1)
    table = jnp.zeros((128, 128), f32)
    for k in range(2):
        table = table + jnp.where(ids_ref[:, k:k + 1] == lane, weight_ref[:, k:k + 1], 0.0)
    route[c, xl] = table
    pl.semaphore_wait(barrier, len(greeted))

    used = [0]
    sent = []

    def send(src, dst, who):
        k = used[0]
        used[0] += 1
        cp = pltpu.make_async_remote_copy(
            src_ref=src, dst_ref=dst, send_sem=ssem.at[k], recv_sem=rsem.at[k],
            device_id=who, device_id_type=MESH)
        cp.start()
        sent.append(cp)
        return cp

    cross = send(at.at[:, xh, y, z], at.at[:, xh, y, z], opposite)
    route_copies = [send(route.at[c, xl], route.at[c, xl], who) for who in (sibling, beside_same, beside_other)]

    def at_chunk(q, stage, i, half=None):
        xs = slice(None) if half is None else half
        if stage == 0:
            return at.at[q, xs, y, i] if q == 0 else at.at[q, xs, i, z]
        return at.at[q, xs, i] if q == 0 else at.at[q, xs, :, i]

    def ring_gather(parts):
        ahead, back, ends = [], [], []
        for axis, chunk in parts:
            i = where_at[axis]
            ahead.append(send(chunk(i), chunk(i), near(axis, 1)))
            back.append(send(chunk(i), chunk(i), near(axis, -1)))
        for n, (axis, chunk) in enumerate(parts):
            i = where_at[axis]
            before, after = (i + 3) % 4, (i + 1) % 4
            ahead[n].wait_recv()
            one = send(chunk(before, 0), chunk(before, 0), near(axis, 1))
            back[n].wait_recv()
            two = send(chunk(after, 1), chunk(after, 1), near(axis, -1))
            ends.append((one, two))
        for one, two in ends:
            one.wait_recv()
            two.wait_recv()

    cross.wait_recv()
    for stage in range(2):
        axes = ("z", "y") if stage == 0 else ("y", "z")
        ring_gather([
            (axes[q], lambda i, half=None, q=q, stage=stage: at_chunk(q, stage, i, half)) for q in range(2)])

    total = jnp.zeros((128, 192), f32)
    low = (lax.broadcasted_iota(jnp.int32, (16, 48, 128), 1) % 8) < 4
    for q in range(2):
        rows = at[q].astype(f32).reshape(16, 2, 48, 128)
        a, b = rows[:, 0], rows[:, 1]
        even = jnp.where(low, a, pltpu.roll(b, 4, 1)).reshape(16, 6, 8, 128)
        unev = jnp.where(low, pltpu.roll(a, 44, 1), b).reshape(16, 6, 8, 128)
        heads = []
        for v in range(6):
            heads.append(even[:, v].reshape(128, 128).astype(bf16))
            heads.append(unev[:, v].reshape(128, 128).astype(bf16))
        total = total + jnp.dot(
            jnp.concatenate(heads, axis=1), wout_ref[q * 1536:(q + 1) * 1536, :], preferred_element_type=f32)
    middle = (hidden_ref[...].astype(f32) + total).astype(bf16).astype(f32)
    mid[:, 128:256] = jnp.zeros((128, 128), f32)
    mid[:, 0:192] = middle

    lane64 = lax.broadcasted_iota(jnp.int32, (64, 128), 1) < 64
    lane128 = lane < 64
    t0, t1 = mid[:, 0:128], mid[:, 128:256]
    whole = jnp.where(odd, jnp.where(lane128, pltpu.roll(t0, 64, 1), pltpu.roll(t1, 64, 1)), t0)
    packed = jnp.where(
        odd,
        jnp.where(lane64, t0[64:128], pltpu.roll(t0[0:64], 64, 1)),
        jnp.where(lane64, t1[0:64], pltpu.roll(t1[64:128], 64, 1)),
    )
    g[0, c, x, y, z] = whole[0:64].astype(bf16)
    g[1, c, x, y, z] = whole[64:128].astype(bf16)
    g[2, c, x, y, z] = packed.astype(bf16)

    def view(ref, lead, order, stage, i, half=None):
        where = []
        for axis in "xyz":
            at_stage = order.index(axis)
            where.append(i if at_stage == stage else slice(None) if at_stage < stage else where_at[axis])
        rows = slice(None) if half is None else pl.ds(half * 32, 32)
        return ref.at[(*lead, *where, rows)]

    passed = []

    def hand_over(q, stage, i):
        v = view(g, (q, c), GATHER_ORDER[q], stage, i)
        passed.append(send(v, v, sibling))

    for stage in range(3):
        parts = [
            (GATHER_ORDER[q][stage],
             lambda i, half=None, q=q, stage=stage: view(g, (q, c), GATHER_ORDER[q], stage, i, half))
            for q in range(3)
        ]
        if stage < 2:
            ring_gather(parts)
            continue
        ahead, back, ends = [], [], []
        for axis, chunk in parts:
            i = where_at[axis]
            ahead.append(send(chunk(i), chunk(i), near(axis, 1)))
            back.append(send(chunk(i), chunk(i), near(axis, -1)))
        for q in range(3):
            hand_over(q, 2, where_at[parts[q][0]])
        for q, (axis, chunk) in enumerate(parts):
            i = where_at[axis]
            before, after = (i + 3) % 4, (i + 1) % 4
            ahead[q].wait_recv()
            one = send(chunk(before, 0), chunk(before, 0), near(axis, 1))
            back[q].wait_recv()
            two = send(chunk(after, 1), chunk(after, 1), near(axis, -1))
            ends.append((one, two))
            hand_over(q, 2, before)
            hand_over(q, 2, after)
        for q, (one, two) in enumerate(ends):
            one.wait_recv()
            two.wait_recv()
            hand_over(q, 2, (where_at[parts[q][0]] + 2) % 4)

    for cp in local[:n_up]:
        cp.wait()

    lane2 = lax.broadcasted_iota(jnp.int32, (2, 64, 128), 2) < 64

    def gate_and_up(plane, hs):
        acc[...] = jnp.zeros((256, 1024), f32)

        @pl.loop(0, 8)
        def _(i):
            xi, yi = i // 4, i % 4
            tiles = []
            for zp in range(2):
                pieces = []
                for zz in range(2):
                    a = g[0:2, plane, pl.ds(2 * xi, 2), yi, 2 * zp + zz]
                    pieces.append(a.reshape(256, 128))
                h0 = g[2, plane, pl.ds(2 * xi, 2), yi, 2 * zp].astype(f32)
                h1 = g[2, plane, pl.ds(2 * xi, 2), yi, 2 * zp + 1].astype(f32)
                upper = jnp.where(lane2, h0, h1).reshape(128, 128)
                lower = pltpu.roll(jnp.where(lane2, h1, h0).reshape(128, 128), 64, 1)
                halves = jnp.concatenate([upper, lower], axis=0).astype(bf16)
                tiles += [pieces[0], halves, pieces[1]]
            lhs = jnp.concatenate(tiles, axis=1)
            rhs = wcat[pl.ds(pl.multiple_of(i * 768, 768), 768), :]
            acc[...] += jnp.dot(lhs, rhs, preferred_element_type=f32)

        lanes = lax.broadcasted_iota(jnp.int32, (64, 128), 1)
        for e in range(2):
            cols = []
            for half in range(2):
                for xi in range(2):
                    t = route[plane, xi, half * 64:(half + 1) * 64, :]
                    cols.append(jnp.sum(jnp.where(lanes == 2 * pool + e, t, 0.0), axis=1, keepdims=True))
            col = jnp.concatenate(cols, axis=0)
            gate = acc[:, e * 512:e * 512 + 256]
            up = acc[:, e * 512 + 256:e * 512 + 512]
            hs[:, e * 256:(e + 1) * 256] = (gate / (1.0 + jnp.exp(-gate)) * up * col).astype(bf16)

    def down(hs, i):
        return jnp.dot(
            hs[...], wd[:, pl.ds(pl.multiple_of(i * 768, 768), 768)], preferred_element_type=f32)

    def parts_of(out):
        got = []
        for zp in range(2):
            tiles = [out[:, zp * 384 + k * 128:zp * 384 + (k + 1) * 128] for k in range(3)]
            upper = tiles[1][0:128].reshape(2, 64, 128)
            lower = pltpu.roll(tiles[1][128:256], 64, 1).reshape(2, 64, 128)
            got.append((tiles[0].reshape(2, 2, 64, 128), jnp.where(lane2, upper, lower)))
            got.append((tiles[2].reshape(2, 2, 64, 128), jnp.where(lane2, lower, upper)))
        return got

    for cp in route_copies:
        cp.wait_recv()

    gate_and_up(c, hs_mine)
    for cp in passed:
        cp.wait_recv()
    gate_and_up(1 - c, hs_sib)
    for cp in local[n_up:]:
        cp.wait()

    base = used[0]
    used[0] += 8

    def sib_copy(i):
        part = (slice(None), pl.ds(2 * (i // 4), 2), i % 4)
        return pltpu.make_async_remote_copy(
            src_ref=s_sib.at[part], dst_ref=from_sib.at[part], send_sem=ssem.at[base + i],
            recv_sem=rsem.at[base + i], device_id=sibling, device_id_type=MESH)

    @pl.loop(0, 8)
    def _(i):
        xi, yi = i // 4, i % 4
        for zi, (a, h) in enumerate(parts_of(down(hs_sib, i))):
            s_sib[0:2, pl.ds(2 * xi, 2), yi, zi] = a.astype(bf16)
            s_sib[2, pl.ds(2 * xi, 2), yi, zi] = h.astype(bf16)
        sib_copy(i).start()

    @pl.loop(0, 8)
    def _(i):
        xi, yi = i // 4, i % 4
        sib_copy(i).wait_recv()
        for zi, (a, h) in enumerate(parts_of(down(hs_mine, i))):
            fa = from_sib[0:2, pl.ds(2 * xi, 2), yi, zi].astype(f32)
            fh = from_sib[2, pl.ds(2 * xi, 2), yi, zi].astype(f32)
            s_mine[0:2, pl.ds(2 * xi, 2), yi, zi] = (a + fa).astype(bf16)
            s_mine[2, pl.ds(2 * xi, 2), yi, zi] = (h + fh).astype(bf16)

    def chunk_of(q, stage, i, half):
        order = REDUCE_ORDER[q]
        where = []
        for axis in "xyz":
            at_stage = order.index(axis)
            where.append(i if at_stage == stage else slice(None) if at_stage > stage else where_at[axis])
        return s_mine.at[(q, *where, pl.ds(half * 32, 32))]

    for stage, ring in enumerate((ring1, ring2, ring3)):
        firsts, seconds, thirds = [], [], []
        for q in range(3):
            axis = REDUCE_ORDER[q][stage]
            i = where_at[axis]
            before, after, far = (i + 3) % 4, (i + 1) % 4, (i + 2) % 4
            firsts.append((
                send(chunk_of(q, stage, far, 0), ring.at[q, 0], near(axis, 1)),
                send(chunk_of(q, stage, far, 1), ring.at[q, 1], near(axis, -1))))
            seconds.append((
                send(chunk_of(q, stage, after, 1), ring.at[q, 2], near(axis, 1)),
                send(chunk_of(q, stage, before, 0), ring.at[q, 3], near(axis, -1))))
        for q in range(3):
            axis = REDUCE_ORDER[q][stage]
            i = where_at[axis]
            before, after = (i + 3) % 4, (i + 1) % 4
            ahead, back = firsts[q]
            ahead.wait_recv()
            v = chunk_of(q, stage, after, 0)
            v[...] = (v[...].astype(f32) + ring[q, 0].astype(f32)).astype(bf16)
            one = send(v, ring.at[q, 4], near(axis, 1))
            back.wait_recv()
            v = chunk_of(q, stage, before, 1)
            v[...] = (v[...].astype(f32) + ring[q, 1].astype(f32)).astype(bf16)
            two = send(v, ring.at[q, 5], near(axis, -1))
            thirds.append((one, two))
        for q in range(3):
            i = where_at[REDUCE_ORDER[q][stage]]
            for cp in seconds[q] + thirds[q]:
                cp.wait_recv()
            first = (chunk_of(q, stage, i, 0)[...].astype(f32)
                     + ring[q, 4].astype(f32) + ring[q, 3].astype(f32))
            second = (chunk_of(q, stage, i, 1)[...].astype(f32)
                      + ring[q, 2].astype(f32) + ring[q, 5].astype(f32))
            if stage < 2:
                chunk_of(q, stage, i, 0)[...] = first.astype(bf16)
                chunk_of(q, stage, i, 1)[...] = second.astype(bf16)
            else:
                fin[q, 0:32] = first
                fin[q, 32:64] = second

    whole = fin[0:2].reshape(128, 128)
    rolled = pltpu.roll(whole, 64, 1)
    f2 = fin[2]
    r2 = pltpu.roll(f2, 64, 1)
    left = jnp.where(odd, jnp.where(lane128, jnp.concatenate([r2, f2], axis=0), rolled), whole)
    right = jnp.where(odd, rolled, jnp.concatenate([f2, r2], axis=0))
    mid[:, 0:128] += left
    mid[:, 128:256] += right
    out_ref[...] = mid[:, 0:192].astype(bf16)

    for cp in sent:
        cp.wait_send()

    @pl.loop(0, 8)
    def _(i):
        sib_copy(i).wait_send()


def attention(query, new_key, new_value, key_cache, value_cache, lengths):
    local_rows = query.shape[0]
    context = key_cache.shape[1]
    group_size = HEADS // KV_HEADS
    score_scale = HEAD_DIM ** (-0.5)
    queries = query.reshape(local_rows, KV_HEADS, group_size, HEAD_DIM)
    cached_keys = key_cache.reshape(local_rows, context, KV_HEADS, HEAD_DIM)
    cached_values = value_cache.reshape(local_rows, context, KV_HEADS, HEAD_DIM)
    scores = (
        jnp.einsum("rkgd,rtkd->rkgt", queries, cached_keys, preferred_element_type=jnp.float32)
        * score_scale
    )
    usable = (jnp.arange(context)[None, :] < lengths[:, None])[:, None, None, :]
    row_max = jnp.max(jnp.where(usable, scores, floor_value), axis=-1)
    weights = jnp.where(usable, jnp.exp(scores - row_max[..., None]), 0.0)
    weight_total = jnp.sum(weights, axis=-1)
    cache_sum = jnp.einsum(
        "rkgt,rtkd->rkgd",
        weights.astype(jnp.bfloat16),
        cached_values,
        preferred_element_type=jnp.float32,
    )
    fresh_keys = new_key.reshape(local_rows, KV_HEADS, HEAD_DIM)
    fresh_score = (
        jnp.einsum("rkgd,rkd->rkg", queries, fresh_keys, preferred_element_type=jnp.float32)
        * score_scale
    )
    final_max = jnp.maximum(row_max, fresh_score)
    cache_factor = jnp.exp(row_max - final_max)
    fresh_factor = jnp.exp(fresh_score - final_max)
    fresh_values = new_value.reshape(local_rows, KV_HEADS, 1, HEAD_DIM).astype(jnp.float32)
    numerator = cache_sum * cache_factor[..., None] + fresh_factor[..., None] * fresh_values
    attended = numerator / (weight_total * cache_factor + fresh_factor)[..., None]
    return attended.astype(jnp.bfloat16)


def shards(
    query,
    new_key,
    new_value,
    key_cache,
    value_cache,
    lengths,
    hidden_in,
    w_out,
    expert_ids,
    gate_weights,
    w_gate,
    w_up,
    w_down,
):
    attended = attention(query, new_key, new_value, key_cache, value_cache, lengths)
    attended = attended.reshape(4, HEADS, HEAD_DIM).transpose(1, 0, 2).reshape(96, HEAD_DIM)
    bf16, f32 = jnp.bfloat16, jnp.float32
    vmem = pl.BlockSpec(memory_space=pltpu.VMEM)
    hbm = pl.BlockSpec(memory_space=pl.ANY)
    return pl.pallas_call(
        layer_kernel,
        out_shape=jax.ShapeDtypeStruct((128, 192), bf16),
        in_specs=[vmem] * 5 + [hbm] * 3,
        out_specs=vmem,
        scratch_shapes=[
            pltpu.VMEM((WIDTH, 4 * UNITS), bf16),
            pltpu.VMEM((2 * UNITS, WIDTH), bf16),
            pltpu.VMEM((2, 2, 4, 4, 48, 128), bf16),
            pltpu.VMEM((3, 2, 4, 4, 4, 64, 128), bf16),
            pltpu.VMEM((2, 2, 128, 128), f32),
            pltpu.VMEM((3, 4, 4, 4, 64, 128), bf16),
            pltpu.VMEM((3, 4, 4, 4, 64, 128), bf16),
            pltpu.VMEM((3, 4, 4, 4, 64, 128), bf16),
            pltpu.VMEM((3, 6, 4, 4, 32, 128), bf16),
            pltpu.VMEM((3, 6, 4, 32, 128), bf16),
            pltpu.VMEM((3, 6, 32, 128), bf16),
            pltpu.VMEM((256, 1024), f32),
            pltpu.VMEM((256, 512), bf16),
            pltpu.VMEM((256, 512), bf16),
            pltpu.VMEM((128, 256), f32),
            pltpu.VMEM((3, 64, 128), f32),
            pltpu.SemaphoreType.DMA((10,)),
            pltpu.SemaphoreType.DMA((144,)),
            pltpu.SemaphoreType.DMA((144,)),
        ],
        compiler_params=pltpu.CompilerParams(
            collective_id=0, has_side_effects=True, vmem_limit_bytes=60 * 1024 * 1024
        ),
        cost_estimate=pl.CostEstimate(flops=10_000_000_000, bytes_accessed=20_000_000, transcendentals=0),
        name="layer",
    )(attended, expert_ids, gate_weights, hidden_in, w_out, w_gate, w_up, w_down)


def solution(mesh):
    return jax.shard_map(
        shards,
        mesh=mesh,
        in_specs=(
            P(("pool", "dev"), None),
            P(("pool", "dev"), None),
            P(("pool", "dev"), None),
            P(("pool", "dev"), None, None),
            P(("pool", "dev"), None, None),
            P(("pool", "dev")),
            P("pool", "dev"),
            P(None, "dev"),
            P("pool", None),
            P("pool", None),
            P("pool", None, "dev"),
            P("pool", None, "dev"),
            P("pool", "dev", None),
        ),
        out_specs=P("pool", "dev"),
        check_vma=False,
    )
```

```python
import jax
import jax.numpy as jnp
from jax import lax
from jax.experimental import pallas as pl
from jax.experimental.pallas import tpu as pltpu
from jax.sharding import PartitionSpec as P

WIDTH = 6144
UNITS = 256
HEADS = 24
CONTEXT = 512

MESH = pl.DeviceIdType.MESH
floor_value = -1e30

GATHER_ORDER = ("zyx", "yxz", "xzy")
REDUCE_ORDER = ("xyz", "zxy", "yzx")
STEPS = (1, 3, 2)


def layer_kernel(
    len_ref, query_hbm, new_key_hbm, new_value_hbm, ids_hbm, weight_hbm, hidden_hbm,
    key_hbm, value_hbm, wout_hbm, wg_hbm, wu_hbm, wd_hbm,
    out_ref,
    query, new_key, new_value, ids, weight, hidden, keys, values, wout,
    wcat, wd, heads_in, heads_out, at, g, route, route_col, s, from_sib, ring1, ring2, ring3, acc, hs, mid, fin,
    lsem, ssem, rsem,
):
    f32, bf16 = jnp.float32, jnp.bfloat16
    pool, dev = lax.axis_index("pool"), lax.axis_index("dev")
    xl, c = pool // 2, pool % 2
    xh, y, z = dev // 16, (dev // 4) % 4, dev % 4
    x = 2 * xh + xl
    odd = (z % 2) == 1
    where_at = {"x": x, "y": y, "z": z}

    def ident(x_, y_, z_, c_):
        return ((x_ % 2) * 2 + c_, (x_ // 2) * 16 + y_ * 4 + z_)

    def near(**steps):
        p = {a: (where_at[a] + steps.get(a, 0)) % 4 for a in "xyz"}
        return ident(p["x"], p["y"], p["z"], c)

    sibling = ident(x, y, z, 1 - c)
    beside = x + 1 - 2 * xl
    beside_same = ident(beside, y, z, c)
    beside_other = ident(beside, y, z, 1 - c)

    barrier = pltpu.get_barrier_semaphore()
    greeted = [near(**{a: d}) for a in "xyz" for d in STEPS]
    greeted += [near(**{"x": 2, a: d}) for a in "yz" for d in STEPS]
    greeted += [sibling, beside_other]
    for who in greeted:
        pl.semaphore_signal(barrier, inc=1, device_id=who, device_id_type=MESH)

    local = []

    def fetch(src, dst):
        cp = pltpu.make_async_copy(src, dst, lsem.at[len(local)])
        cp.start()
        local.append(cp)

    for src, dst in ((query_hbm, query), (new_key_hbm, new_key), (new_value_hbm, new_value)):
        fetch(src, dst)
    for r in range(4):
        fetch(key_hbm.at[r], keys.at[r])
    for r in range(4):
        fetch(value_hbm.at[r], values.at[r])
    n_att = len(local)
    for src, dst in ((ids_hbm, ids), (weight_hbm, weight), (hidden_hbm, hidden), (wout_hbm, wout)):
        fetch(src, dst)
    n_mid = len(local)
    for e in range(2):
        for half in range(2):
            rows = pl.ds(half * (WIDTH // 2), WIDTH // 2)
            fetch(wg_hbm.at[e, rows], wcat.at[rows, pl.ds(e * 512, UNITS)])
            fetch(wu_hbm.at[e, rows], wcat.at[rows, pl.ds(e * 512 + UNITS, UNITS)])
    n_up = len(local)
    for e in range(2):
        fetch(wd_hbm.at[e], wd.at[pl.ds(e * UNITS, UNITS)])

    for cp in local[:3]:
        cp.wait()
    for h in range(HEADS):
        heads_in[h * 4:(h + 1) * 4, :] = query[:, h * 128:(h + 1) * 128].astype(f32)
    own = (lax.broadcasted_iota(jnp.int32, (HEADS, 512), 0) // 6) == (
        lax.broadcasted_iota(jnp.int32, (HEADS, 512), 1) // 128)
    position = lax.broadcasted_iota(jnp.int32, (HEADS, CONTEXT), 1)
    scale = 128 ** -0.5
    fresh_keys, fresh_values = new_key[...].astype(f32), new_value[...].astype(f32)
    spread, scores, fresh_scores, stats, sums = [], [], [], [], []
    for r in range(4):
        q1 = heads_in[pl.ds(r, HEADS, stride=4), :]
        spread.append(jnp.where(own, jnp.concatenate([q1] * 4, axis=1), 0.0))
        fresh_scores.append(jnp.sum(spread[r] * fresh_keys[r:r + 1, :], axis=1, keepdims=True) * scale)
    for r in range(4):
        local[3 + r].wait()
    for r in range(4):
        scores.append(lax.dot_general(
            spread[r].astype(bf16), keys[r], (((1,), (1,)), ((), ())), preferred_element_type=f32) * scale)
    for r in range(4):
        local[7 + r].wait()
    for r in range(4):
        usable = position < len_ref[r]
        row_max = jnp.max(jnp.where(usable, scores[r], floor_value), axis=1, keepdims=True)
        weights = jnp.where(usable, jnp.exp(scores[r] - row_max), 0.0)
        stats.append((row_max, jnp.sum(weights, axis=1, keepdims=True)))
        sums.append(jnp.dot(weights.astype(bf16), values[r], preferred_element_type=f32))
    for r in range(4):
        row_max, weight_total = stats[r]
        final_max = jnp.maximum(row_max, fresh_scores[r])
        cache_factor = jnp.exp(row_max - final_max)
        fresh_factor = jnp.exp(fresh_scores[r] - final_max)
        numerator = jnp.where(own, sums[r] * cache_factor + fresh_factor * fresh_values[r:r + 1, :], 0.0)
        numerator = (numerator[:, 0:128] + numerator[:, 128:256]) + (numerator[:, 256:384] + numerator[:, 384:512])
        heads_out[pl.ds(r, HEADS, stride=4), :] = numerator / (weight_total * cache_factor + fresh_factor)
    at[0, xh, y, z] = heads_out[0:48].astype(bf16)
    at[1, xh, y, z] = heads_out[48:96].astype(bf16)

    used = [0]
    sent = []

    def remote(src, dst, k, who):
        return pltpu.make_async_remote_copy(
            src_ref=src, dst_ref=dst, send_sem=ssem.at[k], recv_sem=rsem.at[k],
            device_id=who, device_id_type=MESH)

    def send(src, dst, who):
        k = used[0]
        used[0] += 1
        cp = remote(src, dst, k, who)
        cp.start()
        sent.append(cp)
        return cp

    pl.semaphore_wait(barrier, len(greeted))
    first, second = ("z", "y"), ("y", "z")
    arriving = []
    for q in range(2):
        block = at.at[q, xh, y, z]
        for dx in (0, 2):
            for d in (0, *STEPS):
                if dx or d:
                    arriving.append(send(block, block, near(**{"x": dx, first[q]: d})))

    for cp in local[n_att:n_mid]:
        cp.wait()
    expert = lax.broadcasted_iota(jnp.int32, (8, 128), 0)
    table = jnp.zeros((8, 128), f32)
    for k in range(2):
        table = table + jnp.where(ids[k:k + 1, :] == expert, weight[k:k + 1, :], 0.0)
    route[c, xl] = table
    route_copies = [send(route.at[c, xl], route.at[c, xl], who) for who in (sibling, beside_same, beside_other)]

    mid[:, 0:128] = hidden[0:128, :].astype(f32).T
    mid[:, 128:256] = jnp.concatenate([hidden[128:192, :].astype(f32), jnp.zeros((64, 128), f32)], axis=0).T

    for cp in arriving:
        cp.wait_recv()
    arriving = []
    for q in range(2):
        block = at.at[q, :, y] if q == 0 else at.at[q, :, :, z]
        arriving += [send(block, block, near(**{second[q]: d})) for d in STEPS]

    for cp in route_copies:
        cp.wait_recv()
    for e in range(2):
        for cc in range(2):
            for xi in range(2):
                row = jnp.sum(jnp.where(expert == 2 * pool + e, route[cc, xi], 0.0), axis=0, keepdims=True)
                col = jnp.broadcast_to(row, (128, 128)).T
                for t in range(2):
                    for half in range(2):
                        start = half * 128 + cc * 64 + xi * 32
                        route_col[e, t, start:start + 32, :] = col[t * 64 + half * 32:t * 64 + half * 32 + 32]

    for cp in arriving:
        cp.wait_recv()

    total = jnp.zeros((128, 192), f32)
    low = (lax.broadcasted_iota(jnp.int32, (16, 48, 128), 1) % 8) < 4
    for q in range(2):
        rows = at[q].astype(f32).reshape(16, 2, 48, 128)
        a, b = rows[:, 0], rows[:, 1]
        even = jnp.where(low, a, pltpu.roll(b, 4, 1)).reshape(16, 6, 8, 128)
        unev = jnp.where(low, pltpu.roll(a, 44, 1), b).reshape(16, 6, 8, 128)
        heads = []
        for v in range(6):
            heads.append(even[:, v].reshape(128, 128).astype(bf16))
            heads.append(unev[:, v].reshape(128, 128).astype(bf16))
        total = total + lax.dot_general(
            jnp.concatenate(heads, axis=1), wout[:, q * 1536:(q + 1) * 1536],
            (((1,), (1,)), ((), ())), preferred_element_type=f32)
    mid[:, 0:192] = (mid[:, 0:192] + total).astype(bf16).astype(f32)

    lane = lax.broadcasted_iota(jnp.int32, (128, 128), 1) < 64
    lane32 = lax.broadcasted_iota(jnp.int32, (32, 128), 1) < 64
    lane64 = lax.broadcasted_iota(jnp.int32, (64, 128), 1) < 64

    def view(ref, lead, order, stage, i, open_before):
        where = []
        for axis in "xyz":
            k = order.index(axis)
            is_open = k < stage if open_before else k > stage
            where.append(i if k == stage else slice(None) if is_open else where_at[axis])
        return ref.at[(*lead, *where)]

    def gather_view(t, q, stage, i):
        return view(g, (t, q, c), GATHER_ORDER[q], stage, i, True)

    last_at, pass_at, sib_at, sum_at = 60, 78, 102, 118

    def gather_copy(t, stage, q, n, k):
        axis, d = GATHER_ORDER[q][stage], STEPS[n]
        block = gather_view(t, q, stage, where_at[axis])
        return remote(block, block, k, near(**{axis: d}))

    def last_copy(t, q, n):
        return gather_copy(t, 2, q, n, last_at + t * 9 + q * 3 + n)

    def pass_copy(t, q, n):
        back = ((0, *STEPS)[n])
        block = gather_view(t, q, 2, (where_at[GATHER_ORDER[q][2]] + 4 - back) % 4)
        return remote(block, block, pass_at + t * 12 + q * 4 + n, sibling)

    def gather_start(t, stage):
        got = []
        for q in range(3):
            for n in range(3):
                axis = GATHER_ORDER[q][stage]
                block = gather_view(t, q, stage, where_at[axis])
                got.append(send(block, block, near(**{axis: STEPS[n]})))
        return got

    t0, t1 = mid[:, 0:128], mid[:, 128:256]
    whole = jnp.where(odd, jnp.where(lane, pltpu.roll(t0, 64, 1), pltpu.roll(t1, 64, 1)), t0)
    flight = []
    for t in range(2):
        a, b = t0[t * 64:(t + 1) * 64], t1[t * 64:(t + 1) * 64]
        packed = jnp.where(
            odd,
            jnp.where(lane32, a[32:64], pltpu.roll(a[0:32], 64, 1)),
            jnp.where(lane32, b[0:32], pltpu.roll(b[32:64], 64, 1)),
        )
        g[t, 0, c, x, y, z] = whole[t * 64:t * 64 + 32].astype(bf16)
        g[t, 1, c, x, y, z] = whole[t * 64 + 32:t * 64 + 64].astype(bf16)
        g[t, 2, c, x, y, z] = packed.astype(bf16)
        flight.append(gather_start(t, 0))
    for t in range(2):
        for cp in flight[t]:
            cp.wait_recv()
        flight[t] = gather_start(t, 1)
    for t in range(2):
        for cp in flight[t]:
            cp.wait_recv()
        for q in range(3):
            for n in range(3):
                last_copy(t, q, n).start()
        for q in range(3):
            pass_copy(t, q, 0).start()
    assert used[0] <= last_at

    def gather_end(t):
        for n in range(3):
            for q in range(3):
                last_copy(t, q, n).wait_recv()
                pass_copy(t, q, n + 1).start()

    def gate_and_up(t):
        acc[...] = jnp.zeros((256, 1024), f32)

        @pl.loop(0, 8, unroll=8)
        def _(i):
            xi, yi = i // 4, i % 4
            tiles = []
            for zp in range(2):
                pieces = []
                for zz in range(2):
                    pieces.append(g[t, 0:2, :, pl.ds(2 * xi, 2), yi, 2 * zp + zz].reshape(256, 128))
                h0 = g[t, 2, :, pl.ds(2 * xi, 2), yi, 2 * zp].astype(f32).reshape(128, 128)
                h1 = g[t, 2, :, pl.ds(2 * xi, 2), yi, 2 * zp + 1].astype(f32).reshape(128, 128)
                upper = jnp.where(lane, h0, h1)
                lower = pltpu.roll(jnp.where(lane, h1, h0), 64, 1)
                halves = jnp.concatenate([upper, lower], axis=0).astype(bf16)
                tiles += [pieces[0], halves, pieces[1]]
            lhs = jnp.concatenate(tiles, axis=1)
            rhs = wcat[pl.ds(pl.multiple_of(i * 768, 768), 768), :]
            acc[...] += jnp.dot(lhs, rhs, preferred_element_type=f32)

        for e in range(2):
            col = route_col[e, t]
            for k in range(2):
                gate = acc[:, e * 512 + k * 128:e * 512 + (k + 1) * 128]
                up = acc[:, e * 512 + 256 + k * 128:e * 512 + 256 + (k + 1) * 128]
                hs[:, e * 256 + k * 128:e * 256 + (k + 1) * 128] = (
                    gate / (1.0 + jnp.exp(-gate)) * up * col).astype(bf16)

    def sib_copy(t, i):
        part = (pl.ds(2 * (i // 4), 2), i % 4)
        return pltpu.make_async_remote_copy(
            src_ref=s.at[(t, slice(None), 1 - c, *part)], dst_ref=from_sib.at[(t, slice(None), *part)],
            send_sem=ssem.at[sib_at + 8 * t + i], recv_sem=rsem.at[sib_at + 8 * t + i],
            device_id=sibling, device_id_type=MESH)

    def down(t):
        @pl.loop(0, 8, unroll=8)
        def _(i):
            xi, yi = i // 4, i % 4
            out = jnp.dot(
                hs[...], wd[:, pl.ds(pl.multiple_of(i * 768, 768), 768)], preferred_element_type=f32)
            for zp in range(2):
                tiles = [out[:, zp * 384 + k * 128:zp * 384 + (k + 1) * 128] for k in range(3)]
                upper = tiles[1][0:128]
                lower = pltpu.roll(tiles[1][128:256], 64, 1)
                halves = (jnp.where(lane, upper, lower), jnp.where(lane, lower, upper))
                for zz in range(2):
                    there = (pl.ds(2 * xi, 2), yi, 2 * zp + zz)
                    s[(t, pl.ds(0, 2), slice(None), *there)] = tiles[2 * zz].astype(bf16).reshape(2, 2, 2, 32, 128)
                    s[(t, 2, slice(None), *there)] = halves[zz].astype(bf16).reshape(2, 2, 32, 128)
            sib_copy(t, i).start()

    def add_sibling(t):
        @pl.loop(0, 8, unroll=8)
        def _(i):
            part = (pl.ds(2 * (i // 4), 2), i % 4)
            sib_copy(t, i).wait_recv()
            mine = s[(t, slice(None), c, *part)].astype(f32)
            other = from_sib[(t, slice(None), *part)].astype(f32)
            s[(t, slice(None), c, *part)] = (mine + other).astype(bf16)

    rings = (ring1, ring2, ring3)

    def sum_view(t, q, stage, i):
        return view(s, (t, q, c), REDUCE_ORDER[q], stage, i, False)

    def sum_copy(t, stage, q, n):
        axis, d = REDUCE_ORDER[q][stage], STEPS[n]
        return remote(
            sum_view(t, q, stage, (where_at[axis] + d) % 4), rings[stage].at[t, q, n],
            sum_at + t * 27 + stage * 9 + q * 3 + n, near(**{axis: d}))

    def sum_start(t, stage):
        for q in range(3):
            for n in range(3):
                sum_copy(t, stage, q, n).start()

    def sum_end(t, stage):
        for q in range(3):
            for n in range(3):
                sum_copy(t, stage, q, n).wait_recv()
            v = sum_view(t, q, stage, where_at[REDUCE_ORDER[q][stage]])
            r = rings[stage]
            added = (v[...].astype(f32) + r[t, q, 0].astype(f32)) + (r[t, q, 1].astype(f32) + r[t, q, 2].astype(f32))
            if stage < 2:
                v[...] = added.astype(bf16)
            else:
                fin[t, q] = added

    for cp in local[n_mid:]:
        cp.wait()
    gather_end(0)

    @pl.loop(0, 2)
    def _(t):
        for q in range(3):
            for n in range(4):
                pass_copy(t, q, n).wait_recv()
        gate_and_up(t)

        @pl.when(t == 0)
        def _():
            gather_end(1)

        @pl.when(t == 1)
        def _():
            add_sibling(0)
            sum_start(0, 0)

        down(t)

    add_sibling(1)
    sum_start(1, 0)
    for stage in range(3):
        for t in range(2):
            sum_end(t, stage)
            if stage < 2:
                sum_start(t, stage + 1)

    for t in range(2):
        whole = fin[t, 0:2].reshape(64, 128)
        rolled = pltpu.roll(whole, 64, 1)
        f2 = fin[t, 2]
        r2 = pltpu.roll(f2, 64, 1)
        rows = slice(t * 64, (t + 1) * 64)
        mid[rows, 0:128] += jnp.where(
            odd, jnp.where(lane64, jnp.concatenate([r2, f2], axis=0), rolled), whole)
        mid[rows, 128:256] += jnp.where(odd, rolled, jnp.concatenate([f2, r2], axis=0))
    out_ref[0:128, :] = mid[:, 0:128].T.astype(bf16)
    out_ref[128:192, :] = mid[:, 128:256].T[0:64].astype(bf16)

    for cp in sent:
        cp.wait_send()
    for q in range(3):
        for n in range(3):
            last_copy(0, q, n).wait_send()
            last_copy(1, q, n).wait_send()

    @pl.loop(0, 2)
    def _(t):
        for q in range(3):
            for n in range(4):
                pass_copy(t, q, n).wait_send()
            for n in range(3):
                for stage in range(3):
                    sum_copy(t, stage, q, n).wait_send()

        @pl.loop(0, 8)
        def _(i):
            sib_copy(t, i).wait_send()


def shards(
    query,
    new_key,
    new_value,
    key_cache,
    value_cache,
    lengths,
    hidden_in,
    w_out,
    expert_ids,
    gate_weights,
    w_gate,
    w_up,
    w_down,
):
    bf16, f32 = jnp.bfloat16, jnp.float32
    hbm = pl.BlockSpec(memory_space=pl.ANY)
    mixed = pl.pallas_call(
        layer_kernel,
        out_shape=jax.ShapeDtypeStruct((192, 128), bf16),
        in_specs=[pl.BlockSpec(memory_space=pltpu.SMEM)] + [hbm] * 12,
        out_specs=pl.BlockSpec(memory_space=pltpu.VMEM),
        scratch_shapes=[
            pltpu.VMEM((4, 3072), bf16),
            pltpu.VMEM((4, 512), bf16),
            pltpu.VMEM((4, 512), bf16),
            pltpu.VMEM((2, 128), jnp.int32),
            pltpu.VMEM((2, 128), f32),
            pltpu.VMEM((192, 128), bf16),
            pltpu.VMEM((4, CONTEXT, 512), bf16),
            pltpu.VMEM((4, CONTEXT, 512), bf16),
            pltpu.VMEM((192, 3072), bf16),
            pltpu.VMEM((WIDTH, 4 * UNITS), bf16),
            pltpu.VMEM((2 * UNITS, WIDTH), bf16),
            pltpu.VMEM((96, 128), f32),
            pltpu.VMEM((96, 128), f32),
            pltpu.VMEM((2, 2, 4, 4, 48, 128), bf16),
            pltpu.VMEM((2, 3, 2, 4, 4, 4, 32, 128), bf16),
            pltpu.VMEM((2, 2, 8, 128), f32),
            pltpu.VMEM((2, 2, 256, 128), f32),
            pltpu.VMEM((2, 3, 2, 4, 4, 4, 32, 128), bf16),
            pltpu.VMEM((2, 3, 4, 4, 4, 32, 128), bf16),
            pltpu.VMEM((2, 3, 3, 4, 4, 32, 128), bf16),
            pltpu.VMEM((2, 3, 3, 4, 32, 128), bf16),
            pltpu.VMEM((2, 3, 3, 32, 128), bf16),
            pltpu.VMEM((256, 1024), f32),
            pltpu.VMEM((256, 512), bf16),
            pltpu.VMEM((128, 256), f32),
            pltpu.VMEM((2, 3, 32, 128), f32),
            pltpu.SemaphoreType.DMA((26,)),
            pltpu.SemaphoreType.DMA((172,)),
            pltpu.SemaphoreType.DMA((172,)),
        ],
        compiler_params=pltpu.CompilerParams(
            collective_id=0, has_side_effects=True, vmem_limit_bytes=60 * 1024 * 1024
        ),
        cost_estimate=pl.CostEstimate(flops=10_000_000_000, bytes_accessed=25_000_000, transcendentals=0),
        name="layer",
    )(
        lengths, query, new_key, new_value, expert_ids.T, gate_weights.T, hidden_in.T,
        key_cache, value_cache, w_out.T, w_gate, w_up, w_down,
    )
    return mixed.T


def solution(mesh):
    return jax.shard_map(
        shards,
        mesh=mesh,
        in_specs=(
            P(("pool", "dev"), None),
            P(("pool", "dev"), None),
            P(("pool", "dev"), None),
            P(("pool", "dev"), None, None),
            P(("pool", "dev"), None, None),
            P(("pool", "dev")),
            P("pool", "dev"),
            P(None, "dev"),
            P("pool", None),
            P("pool", None),
            P("pool", None, "dev"),
            P("pool", None, "dev"),
            P("pool", "dev", None),
        ),
        out_specs=P("pool", "dev"),
        check_vma=False,
    )
```

```python
import jax
import jax.numpy as jnp
from jax import lax
from jax.experimental import pallas as pl
from jax.experimental.pallas import tpu as pltpu
from jax.sharding import PartitionSpec as P

WIDTH = 6144
UNITS = 256
HEADS = 24
CONTEXT = 512

MESH = pl.DeviceIdType.MESH
floor_value = -1e30

GATHER_ORDER = ("zyx", "yxz", "xzy")
REDUCE_ORDER = ("xyz", "zxy", "yzx")
STEPS = (1, 3, 2)


def layer_kernel(
    len_ref, query_hbm, new_key_hbm, new_value_hbm, ids_hbm, weight_hbm, hidden_hbm,
    key_hbm, value_hbm, wout_hbm, wg_hbm, wu_hbm, wd_hbm,
    out_ref,
    query, new_key, new_value, ids, weight, hidden, keys, values, wout,
    wcat, wd, heads_in, heads_out, at, g, route, route_col, s, from_sib, ring1, ring2, ring3, acc, both, hs, mid, fin,
    lsem, ssem, rsem,
):
    f32, bf16 = jnp.float32, jnp.bfloat16
    pool, dev = lax.axis_index("pool"), lax.axis_index("dev")
    xl, c = pool // 2, pool % 2
    xh, y, z = dev // 16, (dev // 4) % 4, dev % 4
    x = 2 * xh + xl
    odd = (z % 2) == 1
    where_at = {"x": x, "y": y, "z": z}

    def ident(x_, y_, z_, c_):
        return ((x_ % 2) * 2 + c_, (x_ // 2) * 16 + y_ * 4 + z_)

    def near(**steps):
        p = {a: (where_at[a] + steps.get(a, 0)) % 4 for a in "xyz"}
        return ident(p["x"], p["y"], p["z"], c)

    sibling = ident(x, y, z, 1 - c)
    beside = x + 1 - 2 * xl
    beside_same = ident(beside, y, z, c)
    beside_other = ident(beside, y, z, 1 - c)

    barrier = pltpu.get_barrier_semaphore()
    greeted = [near(**{a: d}) for a in "xyz" for d in STEPS]
    greeted += [near(**{"x": 2, a: d}) for a in "yz" for d in STEPS]
    greeted += [sibling, beside_other]

    local = []

    def fetch(src, dst):
        cp = pltpu.make_async_copy(src, dst, lsem.at[len(local)])
        cp.start()
        local.append(cp)

    for src, dst in ((query_hbm, query), (new_key_hbm, new_key), (new_value_hbm, new_value)):
        fetch(src, dst)
    for r in range(4):
        fetch(key_hbm.at[r], keys.at[r])
    for r in range(4):
        fetch(value_hbm.at[r], values.at[r])
    for who in greeted:
        pl.semaphore_signal(barrier, inc=1, device_id=who, device_id_type=MESH)

    for cp in local[:3]:
        cp.wait()
    for h in range(HEADS):
        heads_in[h * 4:(h + 1) * 4, :] = query[:, h * 128:(h + 1) * 128].astype(f32)
    own = (lax.broadcasted_iota(jnp.int32, (HEADS, 512), 0) // 6) == (
        lax.broadcasted_iota(jnp.int32, (HEADS, 512), 1) // 128)
    position = lax.broadcasted_iota(jnp.int32, (HEADS, CONTEXT), 1)
    scale = 128 ** -0.5
    fresh_keys, fresh_values = new_key[...].astype(f32), new_value[...].astype(f32)
    spread, scores, fresh_scores, stats, sums = [], [], [], [], []
    for r in range(4):
        q1 = heads_in[pl.ds(r, HEADS, stride=4), :]
        spread.append(jnp.where(own, jnp.concatenate([q1] * 4, axis=1), 0.0))
        fresh_scores.append(jnp.sum(spread[r] * fresh_keys[r:r + 1, :], axis=1, keepdims=True) * scale)
    for r in range(4):
        local[3 + r].wait()
    for r in range(4):
        scores.append(lax.dot_general(
            spread[r].astype(bf16), keys[r], (((1,), (1,)), ((), ())), preferred_element_type=f32) * scale)
    n_att = len(local)
    for src, dst in ((ids_hbm, ids), (weight_hbm, weight), (hidden_hbm, hidden), (wout_hbm, wout)):
        fetch(src, dst)
    n_mid = len(local)
    for e in range(2):
        for half in range(2):
            rows = pl.ds(half * (WIDTH // 2), WIDTH // 2)
            fetch(wg_hbm.at[e, rows], wcat.at[rows, pl.ds(e * 512, UNITS)])
            fetch(wu_hbm.at[e, rows], wcat.at[rows, pl.ds(e * 512 + UNITS, UNITS)])
    n_up = len(local)
    for e in range(2):
        fetch(wd_hbm.at[e], wd.at[pl.ds(e * UNITS, UNITS)])
    for r in range(4):
        local[7 + r].wait()
    for r in range(4):
        usable = position < len_ref[r]
        row_max = jnp.max(jnp.where(usable, scores[r], floor_value), axis=1, keepdims=True)
        weights = jnp.where(usable, jnp.exp(scores[r] - row_max), 0.0)
        stats.append((row_max, jnp.sum(weights, axis=1, keepdims=True)))
        sums.append(jnp.dot(weights.astype(bf16), values[r], preferred_element_type=f32))
    for r in range(4):
        row_max, weight_total = stats[r]
        final_max = jnp.maximum(row_max, fresh_scores[r])
        cache_factor = jnp.exp(row_max - final_max)
        fresh_factor = jnp.exp(fresh_scores[r] - final_max)
        numerator = jnp.where(own, sums[r] * cache_factor + fresh_factor * fresh_values[r:r + 1, :], 0.0)
        numerator = (numerator[:, 0:128] + numerator[:, 128:256]) + (numerator[:, 256:384] + numerator[:, 384:512])
        heads_out[pl.ds(r, HEADS, stride=4), :] = numerator / (weight_total * cache_factor + fresh_factor)
    at[0, xh, y, z] = heads_out[0:48].astype(bf16)
    at[1, xh, y, z] = heads_out[48:96].astype(bf16)

    used = [0]
    sent = []

    def remote(src, dst, k, who):
        return pltpu.make_async_remote_copy(
            src_ref=src, dst_ref=dst, send_sem=ssem.at[k], recv_sem=rsem.at[k],
            device_id=who, device_id_type=MESH)

    def send(src, dst, who):
        k = used[0]
        used[0] += 1
        cp = remote(src, dst, k, who)
        cp.start()
        sent.append(cp)
        return cp

    pl.semaphore_wait(barrier, len(greeted))
    first, second = ("z", "y"), ("y", "z")
    arriving = []
    for q in range(2):
        block = at.at[q, xh, y, z]
        for dx in (0, 2):
            for d in (0, *STEPS):
                if dx or d:
                    arriving.append(send(block, block, near(**{"x": dx, first[q]: d})))

    for cp in local[n_att:n_mid]:
        cp.wait()
    expert = lax.broadcasted_iota(jnp.int32, (8, 128), 0)
    table = jnp.zeros((8, 128), f32)
    for k in range(2):
        table = table + jnp.where(ids[k:k + 1, :] == expert, weight[k:k + 1, :], 0.0)
    route[c, xl] = table
    route_copies = [send(route.at[c, xl], route.at[c, xl], who) for who in (sibling, beside_same, beside_other)]

    mid[:, 0:128] = hidden[0:128, :].astype(f32).T
    mid[:, 128:256] = jnp.concatenate([hidden[128:192, :].astype(f32), jnp.zeros((64, 128), f32)], axis=0).T

    for cp in arriving:
        cp.wait_recv()
    arriving = []
    for q in range(2):
        block = at.at[q, :, y] if q == 0 else at.at[q, :, :, z]
        arriving += [send(block, block, near(**{second[q]: d})) for d in STEPS]

    for cp in route_copies:
        cp.wait_recv()
    for e in range(2):
        for cc in range(2):
            for xi in range(2):
                row = jnp.sum(jnp.where(expert == 2 * pool + e, route[cc, xi], 0.0), axis=0, keepdims=True)
                col = jnp.broadcast_to(row, (128, 128)).T
                for t in range(2):
                    for half in range(2):
                        start = half * 128 + cc * 64 + xi * 32
                        route_col[e, t, start:start + 32, :] = col[t * 64 + half * 32:t * 64 + half * 32 + 32]

    for cp in arriving:
        cp.wait_recv()

    total = jnp.zeros((128, 192), f32)
    low = (lax.broadcasted_iota(jnp.int32, (16, 48, 128), 1) % 8) < 4
    for q in range(2):
        rows = at[q].astype(f32).reshape(16, 2, 48, 128)
        a, b = rows[:, 0], rows[:, 1]
        even = jnp.where(low, a, pltpu.roll(b, 4, 1)).reshape(16, 6, 8, 128)
        unev = jnp.where(low, pltpu.roll(a, 44, 1), b).reshape(16, 6, 8, 128)
        heads = []
        for v in range(6):
            heads.append(even[:, v].reshape(128, 128).astype(bf16))
            heads.append(unev[:, v].reshape(128, 128).astype(bf16))
        total = total + lax.dot_general(
            jnp.concatenate(heads, axis=1), wout[:, q * 1536:(q + 1) * 1536],
            (((1,), (1,)), ((), ())), preferred_element_type=f32)
    mid[:, 0:192] = (mid[:, 0:192] + total).astype(bf16).astype(f32)

    lane = lax.broadcasted_iota(jnp.int32, (128, 128), 1) < 64
    lane32 = lax.broadcasted_iota(jnp.int32, (32, 128), 1) < 64
    lane64 = lax.broadcasted_iota(jnp.int32, (64, 128), 1) < 64

    def view(ref, lead, order, stage, i, open_before, rows=slice(None)):
        where = []
        for axis in "xyz":
            k = order.index(axis)
            is_open = k < stage if open_before else k > stage
            where.append(i if k == stage else slice(None) if is_open else where_at[axis])
        return ref.at[(*lead, *where, rows)]

    def gather_view(t, q, stage, i, rows=slice(None)):
        return view(g, (t, q, c), GATHER_ORDER[q], stage, i, True, rows)

    last_at, pass_at, sib_at, sum_at, half_at, far_at = 60, 78, 102, 118, 172, 184

    def gather_copy(t, stage, q, n, k):
        axis, d = GATHER_ORDER[q][stage], STEPS[n]
        block = gather_view(t, q, stage, where_at[axis])
        return remote(block, block, k, near(**{axis: d}))

    def last_copy(t, q, n):
        return gather_copy(t, 2, q, n, last_at + t * 9 + q * 3 + n)

    def far_copy(t, q, half):
        axis, d = GATHER_ORDER[q][2], (1, 3)[half]
        block = gather_view(t, q, 2, (where_at[axis] + 4 - d) % 4, pl.ds(half * 16, 16))
        return remote(block, block, far_at + t * 3 + q if half else last_at + t * 9 + q * 3 + 2, near(**{axis: d}))

    def pass_copy(t, q, n):
        back = ((0, *STEPS)[n])
        block = gather_view(t, q, 2, (where_at[GATHER_ORDER[q][2]] + 4 - back) % 4)
        return remote(block, block, pass_at + t * 12 + q * 4 + n, sibling)

    def gather_start(t, stage, q):
        axis = GATHER_ORDER[q][stage]
        block = gather_view(t, q, stage, where_at[axis])
        return [send(block, block, near(**{axis: d})) for d in STEPS]

    t0, t1 = mid[:, 0:128], mid[:, 128:256]
    whole = jnp.where(odd, jnp.where(lane, pltpu.roll(t0, 64, 1), pltpu.roll(t1, 64, 1)), t0)
    flight = []
    for t in range(2):
        a, b = t0[t * 64:(t + 1) * 64], t1[t * 64:(t + 1) * 64]
        packed = jnp.where(
            odd,
            jnp.where(lane32, a[32:64], pltpu.roll(a[0:32], 64, 1)),
            jnp.where(lane32, b[0:32], pltpu.roll(b[32:64], 64, 1)),
        )
        g[t, 0, c, x, y, z] = whole[t * 64:t * 64 + 32].astype(bf16)
        g[t, 1, c, x, y, z] = whole[t * 64 + 32:t * 64 + 64].astype(bf16)
        g[t, 2, c, x, y, z] = packed.astype(bf16)
        flight.append([gather_start(t, 0, q) for q in range(3)])
    for t in range(2):
        for q in range(3):
            for cp in flight[t][q]:
                cp.wait_recv()
            flight[t][q] = gather_start(t, 1, q)
    for t in range(2):
        for q in range(3):
            for cp in flight[t][q]:
                cp.wait_recv()
            for n in range(2):
                last_copy(t, q, n).start()
            pass_copy(t, q, 0).start()
    assert used[0] <= last_at

    def gather_on(t):
        for n in range(2):
            for q in range(3):
                last_copy(t, q, n).wait_recv()
                far_copy(t, q, n).start()
                pass_copy(t, q, n + 1).start()

    def gather_end(t):
        for q in range(3):
            far_copy(t, q, 0).wait_recv()
            far_copy(t, q, 1).wait_recv()
            pass_copy(t, q, 3).start()

    def gate_and_up(t):
        acc[...] = jnp.zeros((256, 1024), f32)

        @pl.loop(0, 8, unroll=8)
        def _(i):
            xi, yi = i // 4, i % 4
            tiles = []
            for zp in range(2):
                pieces = []
                for zz in range(2):
                    pieces.append(g[t, 0:2, :, pl.ds(2 * xi, 2), yi, 2 * zp + zz].reshape(256, 128))
                h0 = g[t, 2, :, pl.ds(2 * xi, 2), yi, 2 * zp].astype(f32).reshape(128, 128)
                h1 = g[t, 2, :, pl.ds(2 * xi, 2), yi, 2 * zp + 1].astype(f32).reshape(128, 128)
                upper = jnp.where(lane, h0, h1)
                lower = pltpu.roll(jnp.where(lane, h1, h0), 64, 1)
                halves = jnp.concatenate([upper, lower], axis=0).astype(bf16)
                tiles += [pieces[0], halves, pieces[1]]
            lhs = jnp.concatenate(tiles, axis=1)
            rhs = wcat[pl.ds(pl.multiple_of(i * 768, 768), 768), :]
            acc[...] += jnp.dot(lhs, rhs, preferred_element_type=f32)

        for e in range(2):
            col = route_col[e, t]
            for k in range(2):
                gate = acc[:, e * 512 + k * 128:e * 512 + (k + 1) * 128]
                up = acc[:, e * 512 + 256 + k * 128:e * 512 + 256 + (k + 1) * 128]
                hs[:, e * 256 + k * 128:e * 256 + (k + 1) * 128] = (
                    gate / (1.0 + jnp.exp(-gate)) * up * col).astype(bf16)

    def sib_copy(t, i):
        part = (pl.ds(2 * (i // 4), 2), i % 4)
        return pltpu.make_async_remote_copy(
            src_ref=s.at[(t, slice(None), 1 - c, *part)], dst_ref=from_sib.at[(t, slice(None), *part)],
            send_sem=ssem.at[sib_at + 8 * t + i], recv_sem=rsem.at[sib_at + 8 * t + i],
            device_id=sibling, device_id_type=MESH)

    def down(t):
        def product(i):
            both[i % 2] = jnp.dot(
                hs[...], wd[:, pl.ds(pl.multiple_of(i * 768, 768), 768)], preferred_element_type=f32)

        def place(i):
            xi, yi = i // 4, i % 4
            for zp in range(2):
                tiles = [both[i % 2, :, zp * 384 + k * 128:zp * 384 + (k + 1) * 128] for k in range(3)]
                upper = tiles[1][0:128]
                lower = pltpu.roll(tiles[1][128:256], 64, 1)
                halves = (jnp.where(lane, upper, lower), jnp.where(lane, lower, upper))
                for zz in range(2):
                    there = (pl.ds(2 * xi, 2), yi, 2 * zp + zz)
                    s[(t, pl.ds(0, 2), slice(None), *there)] = tiles[2 * zz].astype(bf16).reshape(2, 2, 2, 32, 128)
                    s[(t, 2, slice(None), *there)] = halves[zz].astype(bf16).reshape(2, 2, 32, 128)

        product(0)

        @pl.loop(1, 8)
        def _(i):
            place(i - 1)
            product(i)
            sib_copy(t, i - 1).start()

        place(7)
        sib_copy(t, 7).start()

    def add_sibling(t, half):
        @pl.loop(0, 4, unroll=2)
        def _(yi):
            part = (pl.ds(2 * half, 2), yi)
            sib_copy(t, 4 * half + yi).wait_recv()
            s[(t, slice(None), c, *part)] = s[(t, slice(None), c, *part)] + from_sib[(t, slice(None), *part)]

    rings = (ring1, ring2, ring3)

    def sum_view(t, q, stage, i):
        return view(s, (t, q, c), REDUCE_ORDER[q], stage, i, False)

    def sum_copy(t, stage, q, n):
        axis, d = REDUCE_ORDER[q][stage], STEPS[n]
        return remote(
            sum_view(t, q, stage, (where_at[axis] + d) % 4), rings[stage].at[t, q, n],
            sum_at + t * 27 + stage * 9 + q * 3 + n, near(**{axis: d}))

    def half_copy(t, q, n, half):
        axis, d = REDUCE_ORDER[q][0], STEPS[n]
        i = (where_at[axis] + d) % 4
        xs = pl.ds(2 * half, 2)
        src = s.at[t, q, c, xs, :, i] if axis == "z" else s.at[t, q, c, xs, i]
        k = half_at + t * 6 + (q - 1) * 3 + n if half else sum_at + t * 27 + q * 3 + n
        return remote(src, ring1.at[t, q, n, xs], k, near(**{axis: d}))

    def first_sums(t):
        for half in range(2):
            add_sibling(t, half)
            for n in range(3):
                @pl.when((x + STEPS[n]) % 4 // 2 == half)
                def _():
                    sum_copy(t, 0, 0, n).start()
                for q in (1, 2):
                    half_copy(t, q, n, half).start()

    def sum_start(t, stage, q):
        for n in range(3):
            sum_copy(t, stage, q, n).start()

    def sum_end(t, stage, q):
        for n in range(3):
            if stage == 0 and q > 0:
                half_copy(t, q, n, 0).wait_recv()
                half_copy(t, q, n, 1).wait_recv()
            else:
                sum_copy(t, stage, q, n).wait_recv()
        v = sum_view(t, q, stage, where_at[REDUCE_ORDER[q][stage]])
        r = rings[stage]
        added = (v[...].astype(f32) + r[t, q, 0].astype(f32)) + (r[t, q, 1].astype(f32) + r[t, q, 2].astype(f32))
        if stage < 2:
            v[...] = added.astype(bf16)
            sum_start(t, stage + 1, q)
        else:
            fin[t, q] = added

    for cp in local[n_mid:]:
        cp.wait()

    gather_on(0)
    gather_on(1)
    gather_end(0)

    @pl.loop(0, 2)
    def _(t):
        for q in range(3):
            for n in range(4):
                pass_copy(t, q, n).wait_recv()

        gate_and_up(t)

        @pl.when(t == 0)
        def _():
            gather_end(1)

        @pl.when(t == 1)
        def _():
            first_sums(0)

        down(t)

    first_sums(1)

    for cp in sent:
        cp.wait_send()

    @pl.loop(0, 2)
    def _(t):
        for q in range(3):
            for n in range(2):
                last_copy(t, q, n).wait_send()
                far_copy(t, q, n).wait_send()
            for n in range(4):
                pass_copy(t, q, n).wait_send()

        @pl.loop(0, 8)
        def _(i):
            sib_copy(t, i).wait_send()

    def sums_left(stage):
        @pl.loop(0, 2)
        def _(t):
            for q in range(3):
                for n in range(3):
                    if stage == 0 and q > 0:
                        half_copy(t, q, n, 0).wait_send()
                        half_copy(t, q, n, 1).wait_send()
                    else:
                        sum_copy(t, stage, q, n).wait_send()

    for stage in range(3):
        @pl.loop(0, 2)
        def _(t):
            for q in range(3):
                sum_end(t, stage, q)

        if stage < 2:
            sums_left(stage)

    for t in range(2):
        whole = fin[t, 0:2].reshape(64, 128)
        rolled = pltpu.roll(whole, 64, 1)
        f2 = fin[t, 2]
        r2 = pltpu.roll(f2, 64, 1)
        rows = slice(t * 64, (t + 1) * 64)
        mid[rows, 0:128] += jnp.where(
            odd, jnp.where(lane64, jnp.concatenate([r2, f2], axis=0), rolled), whole)
        mid[rows, 128:256] += jnp.where(odd, rolled, jnp.concatenate([f2, r2], axis=0))
    out_ref[0:128, :] = mid[:, 0:128].T.astype(bf16)
    out_ref[128:192, :] = mid[:, 128:256].T[0:64].astype(bf16)

    sums_left(2)


def shards(
    query,
    new_key,
    new_value,
    key_cache,
    value_cache,
    lengths,
    hidden_in,
    w_out,
    expert_ids,
    gate_weights,
    w_gate,
    w_up,
    w_down,
):
    bf16, f32 = jnp.bfloat16, jnp.float32
    hbm = pl.BlockSpec(memory_space=pl.ANY)
    mixed = pl.pallas_call(
        layer_kernel,
        out_shape=jax.ShapeDtypeStruct((192, 128), bf16),
        in_specs=[pl.BlockSpec(memory_space=pltpu.SMEM)] + [hbm] * 12,
        out_specs=pl.BlockSpec(memory_space=pltpu.VMEM),
        scratch_shapes=[
            pltpu.VMEM((4, 3072), bf16),
            pltpu.VMEM((4, 512), bf16),
            pltpu.VMEM((4, 512), bf16),
            pltpu.VMEM((2, 128), jnp.int32),
            pltpu.VMEM((2, 128), f32),
            pltpu.VMEM((192, 128), bf16),
            pltpu.VMEM((4, CONTEXT, 512), bf16),
            pltpu.VMEM((4, CONTEXT, 512), bf16),
            pltpu.VMEM((192, 3072), bf16),
            pltpu.VMEM((WIDTH, 4 * UNITS), bf16),
            pltpu.VMEM((2 * UNITS, WIDTH), bf16),
            pltpu.VMEM((96, 128), f32),
            pltpu.VMEM((96, 128), f32),
            pltpu.VMEM((2, 2, 4, 4, 48, 128), bf16),
            pltpu.VMEM((2, 3, 2, 4, 4, 4, 32, 128), bf16),
            pltpu.VMEM((2, 2, 8, 128), f32),
            pltpu.VMEM((2, 2, 256, 128), f32),
            pltpu.VMEM((2, 3, 2, 4, 4, 4, 32, 128), bf16),
            pltpu.VMEM((2, 3, 4, 4, 4, 32, 128), bf16),
            pltpu.VMEM((2, 3, 3, 4, 4, 32, 128), bf16),
            pltpu.VMEM((2, 3, 3, 4, 32, 128), bf16),
            pltpu.VMEM((2, 3, 3, 32, 128), bf16),
            pltpu.VMEM((256, 1024), f32),
            pltpu.VMEM((2, 256, 768), f32),
            pltpu.VMEM((256, 512), bf16),
            pltpu.VMEM((128, 256), f32),
            pltpu.VMEM((2, 3, 32, 128), f32),
            pltpu.SemaphoreType.DMA((26,)),
            pltpu.SemaphoreType.DMA((190,)),
            pltpu.SemaphoreType.DMA((190,)),
        ],
        compiler_params=pltpu.CompilerParams(
            collective_id=0, has_side_effects=True, vmem_limit_bytes=60 * 1024 * 1024
        ),
        cost_estimate=pl.CostEstimate(flops=10_000_000_000, bytes_accessed=25_000_000, transcendentals=0),
        name="layer",
    )(
        lengths, query, new_key, new_value, expert_ids.T, gate_weights.T, hidden_in.T,
        key_cache, value_cache, w_out.T, w_gate, w_up, w_down,
    )
    return mixed.T


def solution(mesh):
    return jax.shard_map(
        shards,
        mesh=mesh,
        in_specs=(
            P(("pool", "dev"), None),
            P(("pool", "dev"), None),
            P(("pool", "dev"), None),
            P(("pool", "dev"), None, None),
            P(("pool", "dev"), None, None),
            P(("pool", "dev")),
            P("pool", "dev"),
            P(None, "dev"),
            P("pool", None),
            P("pool", None),
            P("pool", None, "dev"),
            P("pool", None, "dev"),
            P("pool", "dev", None),
        ),
        out_specs=P("pool", "dev"),
        check_vma=False,
    )
```

```python
import jax
import jax.numpy as jnp
from jax import lax
from jax.experimental import pallas as pl
from jax.experimental.pallas import tpu as pltpu
from jax.sharding import PartitionSpec as P

WIDTH = 6144
UNITS = 256
HEADS = 24
CONTEXT = 512

MESH = pl.DeviceIdType.MESH
floor_value = -1e30

GATHER_ORDER = ("zyx", "yxz", "xzy")
REDUCE_ORDER = ("xyz", "zxy", "yzx")
STEPS = (1, 3, 2)


def layer_kernel(
    len_ref, query_hbm, new_key_hbm, new_value_hbm, ids_hbm, weight_hbm, hidden_hbm,
    key_hbm, value_hbm, wout_hbm, wg_hbm, wu_hbm, wd_hbm,
    out_ref,
    query, new_key, new_value, ids, weight, hidden, keys, values, wout,
    wcat, wd, heads_in, heads_out, at, g, route, route_col, s, from_sib, ring1, ring2, ring3, acc, both, hs, mid, fin,
    lsem, ssem, rsem,
):
    f32, bf16 = jnp.float32, jnp.bfloat16
    pool, dev = lax.axis_index("pool"), lax.axis_index("dev")
    xl, c = pool // 2, pool % 2
    xh, y, z = dev // 16, (dev // 4) % 4, dev % 4
    x = 2 * xh + xl
    odd = (z % 2) == 1
    where_at = {"x": x, "y": y, "z": z}

    def ident(x_, y_, z_, c_):
        return ((x_ % 2) * 2 + c_, (x_ // 2) * 16 + y_ * 4 + z_)

    def near(**steps):
        p = {a: (where_at[a] + steps.get(a, 0)) % 4 for a in "xyz"}
        return ident(p["x"], p["y"], p["z"], c)

    sibling = ident(x, y, z, 1 - c)
    beside = x + 1 - 2 * xl
    beside_same = ident(beside, y, z, c)
    beside_other = ident(beside, y, z, 1 - c)

    barrier = pltpu.get_barrier_semaphore()
    greeted = [near(**{a: d}) for a in "xyz" for d in STEPS]
    greeted += [near(**{"x": 2, a: d}) for a in "yz" for d in STEPS]
    greeted += [sibling, beside_other]

    local = []

    def fetch(src, dst):
        cp = pltpu.make_async_copy(src, dst, lsem.at[len(local)])
        cp.start()
        local.append(cp)

    for src, dst in ((query_hbm, query), (new_key_hbm, new_key), (new_value_hbm, new_value)):
        fetch(src, dst)
    for r in range(4):
        fetch(key_hbm.at[r], keys.at[r])
    for r in range(4):
        fetch(value_hbm.at[r], values.at[r])
    for who in greeted:
        pl.semaphore_signal(barrier, inc=1, device_id=who, device_id_type=MESH)

    for cp in local[:3]:
        cp.wait()
    for h in range(HEADS):
        heads_in[h * 4:(h + 1) * 4, :] = query[:, h * 128:(h + 1) * 128].astype(f32)
    own = (lax.broadcasted_iota(jnp.int32, (HEADS, 512), 0) // 6) == (
        lax.broadcasted_iota(jnp.int32, (HEADS, 512), 1) // 128)
    position = lax.broadcasted_iota(jnp.int32, (HEADS, CONTEXT), 1)
    scale = 128 ** -0.5
    fresh_keys, fresh_values = new_key[...].astype(f32), new_value[...].astype(f32)
    spread, scores, fresh_scores, stats, sums = [], [], [], [], []
    for r in range(4):
        q1 = heads_in[pl.ds(r, HEADS, stride=4), :]
        spread.append(jnp.where(own, jnp.concatenate([q1] * 4, axis=1), 0.0))
        fresh_scores.append(jnp.sum(spread[r] * fresh_keys[r:r + 1, :], axis=1, keepdims=True) * scale)
    for r in range(4):
        local[3 + r].wait()
    for r in range(4):
        scores.append(lax.dot_general(
            spread[r].astype(bf16), keys[r], (((1,), (1,)), ((), ())), preferred_element_type=f32) * scale)
    n_att = len(local)
    for src, dst in ((ids_hbm, ids), (weight_hbm, weight), (hidden_hbm, hidden), (wout_hbm, wout)):
        fetch(src, dst)
    n_mid = len(local)
    for e in range(2):
        for half in range(2):
            rows = pl.ds(half * (WIDTH // 2), WIDTH // 2)
            fetch(wg_hbm.at[e, rows], wcat.at[rows, pl.ds(e * 512, UNITS)])
            fetch(wu_hbm.at[e, rows], wcat.at[rows, pl.ds(e * 512 + UNITS, UNITS)])
    n_up = len(local)
    for e in range(2):
        fetch(wd_hbm.at[e], wd.at[pl.ds(e * UNITS, UNITS)])
    for r in range(4):
        local[7 + r].wait()
    for r in range(4):
        usable = position < len_ref[r]
        row_max = jnp.max(jnp.where(usable, scores[r], floor_value), axis=1, keepdims=True)
        weights = jnp.where(usable, jnp.exp(scores[r] - row_max), 0.0)
        stats.append((row_max, jnp.sum(weights, axis=1, keepdims=True)))
        sums.append(jnp.dot(weights.astype(bf16), values[r], preferred_element_type=f32))
    for r in range(4):
        row_max, weight_total = stats[r]
        final_max = jnp.maximum(row_max, fresh_scores[r])
        cache_factor = jnp.exp(row_max - final_max)
        fresh_factor = jnp.exp(fresh_scores[r] - final_max)
        numerator = jnp.where(own, sums[r] * cache_factor + fresh_factor * fresh_values[r:r + 1, :], 0.0)
        numerator = (numerator[:, 0:128] + numerator[:, 128:256]) + (numerator[:, 256:384] + numerator[:, 384:512])
        heads_out[pl.ds(r, HEADS, stride=4), :] = numerator / (weight_total * cache_factor + fresh_factor)
    at[0, xh, y, z] = heads_out[0:48].astype(bf16)
    at[1, xh, y, z] = heads_out[48:96].astype(bf16)

    used = [0]
    sent = []

    def remote(src, dst, k, who):
        return pltpu.make_async_remote_copy(
            src_ref=src, dst_ref=dst, send_sem=ssem.at[k], recv_sem=rsem.at[k],
            device_id=who, device_id_type=MESH)

    def send(src, dst, who):
        k = used[0]
        used[0] += 1
        cp = remote(src, dst, k, who)
        cp.start()
        sent.append(cp)
        return cp

    pl.semaphore_wait(barrier, len(greeted))
    first, second = ("z", "y"), ("y", "z")
    arriving = [[], []]
    for q in range(2):
        block = at.at[q, xh, y, z]
        for dx in (0, 2):
            for d in (0, *STEPS):
                if dx or d:
                    arriving[q].append(send(block, block, near(**{"x": dx, first[q]: d})))

    for cp in local[n_att:n_mid]:
        cp.wait()
    expert = lax.broadcasted_iota(jnp.int32, (8, 128), 0)
    table = jnp.zeros((8, 128), f32)
    for k in range(2):
        table = table + jnp.where(ids[k:k + 1, :] == expert, weight[k:k + 1, :], 0.0)
    route[c, xl] = table
    route_copies = [send(route.at[c, xl], route.at[c, xl], who) for who in (sibling, beside_same, beside_other)]

    mid[:, 0:128] = hidden[0:128, :].astype(f32).T
    mid[:, 128:256] = jnp.concatenate([hidden[128:192, :].astype(f32), jnp.zeros((64, 128), f32)], axis=0).T

    for q in range(2):
        for cp in arriving[q]:
            cp.wait_recv()
        block = at.at[q, :, y] if q == 0 else at.at[q, :, :, z]
        arriving[q] = [send(block, block, near(**{second[q]: d})) for d in STEPS]

    for cp in route_copies:
        cp.wait_recv()
    for e in range(2):
        for cc in range(2):
            for xi in range(2):
                row = jnp.sum(jnp.where(expert == 2 * pool + e, route[cc, xi], 0.0), axis=0, keepdims=True)
                col = jnp.broadcast_to(row, (128, 128)).T
                for t in range(2):
                    for half in range(2):
                        start = half * 128 + cc * 64 + xi * 32
                        route_col[e, t, start:start + 32, :] = col[t * 64 + half * 32:t * 64 + half * 32 + 32]

    total = jnp.zeros((128, 192), f32)
    low = (lax.broadcasted_iota(jnp.int32, (16, 48, 128), 1) % 8) < 4
    for q in range(2):
        for cp in arriving[q]:
            cp.wait_recv()
        rows = at[q].astype(f32).reshape(16, 2, 48, 128)
        a, b = rows[:, 0], rows[:, 1]
        even = jnp.where(low, a, pltpu.roll(b, 4, 1)).reshape(16, 6, 8, 128)
        unev = jnp.where(low, pltpu.roll(a, 44, 1), b).reshape(16, 6, 8, 128)
        heads = []
        for v in range(6):
            heads.append(even[:, v].reshape(128, 128).astype(bf16))
            heads.append(unev[:, v].reshape(128, 128).astype(bf16))
        total = total + lax.dot_general(
            jnp.concatenate(heads, axis=1), wout[:, q * 1536:(q + 1) * 1536],
            (((1,), (1,)), ((), ())), preferred_element_type=f32)
    mid[:, 0:192] = (mid[:, 0:192] + total).astype(bf16).astype(f32)

    lane = lax.broadcasted_iota(jnp.int32, (128, 128), 1) < 64
    lane32 = lax.broadcasted_iota(jnp.int32, (32, 128), 1) < 64
    lane64 = lax.broadcasted_iota(jnp.int32, (64, 128), 1) < 64

    def view(ref, lead, order, stage, i, open_before, rows=slice(None)):
        where = []
        for axis in "xyz":
            k = order.index(axis)
            is_open = k < stage if open_before else k > stage
            where.append(i if k == stage else slice(None) if is_open else where_at[axis])
        return ref.at[(*lead, *where, rows)]

    def gather_view(t, q, stage, i, rows=slice(None)):
        return view(g, (t, q, c), GATHER_ORDER[q], stage, i, True, rows)

    last_at, pass_at, sib_at, sum_at, half_at, far_at = 60, 78, 102, 118, 172, 184

    def gather_copy(t, stage, q, n, k):
        axis, d = GATHER_ORDER[q][stage], STEPS[n]
        block = gather_view(t, q, stage, where_at[axis])
        return remote(block, block, k, near(**{axis: d}))

    def last_copy(t, q, n):
        return gather_copy(t, 2, q, n, last_at + t * 9 + q * 3 + n)

    def far_copy(t, q, half):
        axis, d = GATHER_ORDER[q][2], (1, 3)[half]
        block = gather_view(t, q, 2, (where_at[axis] + 4 - d) % 4, pl.ds(half * 16, 16))
        return remote(block, block, far_at + t * 3 + q if half else last_at + t * 9 + q * 3 + 2, near(**{axis: d}))

    def pass_copy(t, q, n):
        back = ((0, *STEPS)[n])
        block = gather_view(t, q, 2, (where_at[GATHER_ORDER[q][2]] + 4 - back) % 4)
        return remote(block, block, pass_at + t * 12 + q * 4 + n, sibling)

    def gather_start(t, stage, q):
        axis = GATHER_ORDER[q][stage]
        block = gather_view(t, q, stage, where_at[axis])
        return [send(block, block, near(**{axis: d})) for d in STEPS]

    t0, t1 = mid[:, 0:128], mid[:, 128:256]
    whole = jnp.where(odd, jnp.where(lane, pltpu.roll(t0, 64, 1), pltpu.roll(t1, 64, 1)), t0)
    flight = []
    for t in range(2):
        a, b = t0[t * 64:(t + 1) * 64], t1[t * 64:(t + 1) * 64]
        packed = jnp.where(
            odd,
            jnp.where(lane32, a[32:64], pltpu.roll(a[0:32], 64, 1)),
            jnp.where(lane32, b[0:32], pltpu.roll(b[32:64], 64, 1)),
        )
        g[t, 0, c, x, y, z] = whole[t * 64:t * 64 + 32].astype(bf16)
        g[t, 1, c, x, y, z] = whole[t * 64 + 32:t * 64 + 64].astype(bf16)
        g[t, 2, c, x, y, z] = packed.astype(bf16)
        flight.append([gather_start(t, 0, q) for q in range(3)])
    for t in range(2):
        for q in range(3):
            for cp in flight[t][q]:
                cp.wait_recv()
            flight[t][q] = gather_start(t, 1, q)
    for t in range(2):
        for q in range(3):
            for cp in flight[t][q]:
                cp.wait_recv()
            for n in range(2):
                last_copy(t, q, n).start()
            pass_copy(t, q, 0).start()
    assert used[0] <= last_at

    def gather_on(t):
        for n in range(2):
            for q in range(3):
                last_copy(t, q, n).wait_recv()
                far_copy(t, q, n).start()
                pass_copy(t, q, n + 1).start()

    def gather_end(t):
        for q in range(3):
            far_copy(t, q, 0).wait_recv()
            far_copy(t, q, 1).wait_recv()
            pass_copy(t, q, 3).start()

    def gate_and_up(t):
        acc[...] = jnp.zeros((256, 1024), f32)

        @pl.loop(0, 8, unroll=8)
        def _(i):
            xi, yi = i // 4, i % 4
            tiles = []
            for zp in range(2):
                pieces = []
                for zz in range(2):
                    pieces.append(g[t, 0:2, :, pl.ds(2 * xi, 2), yi, 2 * zp + zz].reshape(256, 128))
                h0 = g[t, 2, :, pl.ds(2 * xi, 2), yi, 2 * zp].astype(f32).reshape(128, 128)
                h1 = g[t, 2, :, pl.ds(2 * xi, 2), yi, 2 * zp + 1].astype(f32).reshape(128, 128)
                upper = jnp.where(lane, h0, h1)
                lower = pltpu.roll(jnp.where(lane, h1, h0), 64, 1)
                halves = jnp.concatenate([upper, lower], axis=0).astype(bf16)
                tiles += [pieces[0], halves, pieces[1]]
            lhs = jnp.concatenate(tiles, axis=1)
            rhs = wcat[pl.ds(pl.multiple_of(i * 768, 768), 768), :]
            acc[...] += jnp.dot(lhs, rhs, preferred_element_type=f32)

        for e in range(2):
            col = route_col[e, t]
            for k in range(2):
                gate = acc[:, e * 512 + k * 128:e * 512 + (k + 1) * 128]
                up = acc[:, e * 512 + 256 + k * 128:e * 512 + 256 + (k + 1) * 128]
                hs[:, e * 256 + k * 128:e * 256 + (k + 1) * 128] = (
                    gate / (1.0 + jnp.exp(-gate)) * up * col).astype(bf16)

    def sib_copy(t, i):
        part = (pl.ds(2 * (i // 4), 2), i % 4)
        return pltpu.make_async_remote_copy(
            src_ref=s.at[(t, slice(None), 1 - c, *part)], dst_ref=from_sib.at[(t, slice(None), *part)],
            send_sem=ssem.at[sib_at + 8 * t + i], recv_sem=rsem.at[sib_at + 8 * t + i],
            device_id=sibling, device_id_type=MESH)

    def down(t):
        def product(i):
            both[i % 2] = jnp.dot(
                hs[...], wd[:, pl.ds(pl.multiple_of(i * 768, 768), 768)], preferred_element_type=f32)

        def place(i):
            xi, yi = i // 4, i % 4
            for zp in range(2):
                tiles = [both[i % 2, :, zp * 384 + k * 128:zp * 384 + (k + 1) * 128] for k in range(3)]
                upper = tiles[1][0:128]
                lower = pltpu.roll(tiles[1][128:256], 64, 1)
                halves = (jnp.where(lane, upper, lower), jnp.where(lane, lower, upper))
                for zz in range(2):
                    there = (pl.ds(2 * xi, 2), yi, 2 * zp + zz)
                    s[(t, pl.ds(0, 2), slice(None), *there)] = tiles[2 * zz].astype(bf16).reshape(2, 2, 2, 32, 128)
                    s[(t, 2, slice(None), *there)] = halves[zz].astype(bf16).reshape(2, 2, 32, 128)

        product(0)

        @pl.loop(1, 8)
        def _(i):
            place(i - 1)
            product(i)
            sib_copy(t, i - 1).start()

        place(7)
        sib_copy(t, 7).start()

    def add_sibling(t, half):
        @pl.loop(0, 4, unroll=2)
        def _(yi):
            part = (pl.ds(2 * half, 2), yi)
            sib_copy(t, 4 * half + yi).wait_recv()
            s[(t, slice(None), c, *part)] = s[(t, slice(None), c, *part)] + from_sib[(t, slice(None), *part)]

    rings = (ring1, ring2, ring3)

    def sum_view(t, q, stage, i):
        return view(s, (t, q, c), REDUCE_ORDER[q], stage, i, False)

    def sum_copy(t, stage, q, n):
        axis, d = REDUCE_ORDER[q][stage], STEPS[n]
        return remote(
            sum_view(t, q, stage, (where_at[axis] + d) % 4), rings[stage].at[t, q, n],
            sum_at + t * 27 + stage * 9 + q * 3 + n, near(**{axis: d}))

    def half_copy(t, q, n, half):
        axis, d = REDUCE_ORDER[q][0], STEPS[n]
        i = (where_at[axis] + d) % 4
        xs = pl.ds(2 * half, 2)
        src = s.at[t, q, c, xs, :, i] if axis == "z" else s.at[t, q, c, xs, i]
        k = half_at + t * 6 + (q - 1) * 3 + n if half else sum_at + t * 27 + q * 3 + n
        return remote(src, ring1.at[t, q, n, xs], k, near(**{axis: d}))

    def first_sums(t):
        for half in range(2):
            add_sibling(t, half)
            for n in range(3):
                @pl.when((x + STEPS[n]) % 4 // 2 == half)
                def _():
                    sum_copy(t, 0, 0, n).start()
                for q in (1, 2):
                    half_copy(t, q, n, half).start()

    def sum_start(t, stage, q):
        for n in range(3):
            sum_copy(t, stage, q, n).start()

    def sum_end(t, stage, q):
        for n in range(3):
            if stage == 0 and q > 0:
                half_copy(t, q, n, 0).wait_recv()
                half_copy(t, q, n, 1).wait_recv()
            else:
                sum_copy(t, stage, q, n).wait_recv()
        v = sum_view(t, q, stage, where_at[REDUCE_ORDER[q][stage]])
        r = rings[stage]
        added = (v[...].astype(f32) + r[t, q, 0].astype(f32)) + (r[t, q, 1].astype(f32) + r[t, q, 2].astype(f32))
        if stage < 2:
            v[...] = added.astype(bf16)
            sum_start(t, stage + 1, q)
        else:
            fin[t, q] = added

    for cp in local[n_mid:]:
        cp.wait()

    gather_on(0)
    gather_on(1)
    gather_end(0)

    @pl.loop(0, 2)
    def _(t):
        for q in range(3):
            for n in range(4):
                pass_copy(t, q, n).wait_recv()

        gate_and_up(t)

        @pl.when(t == 0)
        def _():
            gather_end(1)

        @pl.when(t == 1)
        def _():
            first_sums(0)

        down(t)

    first_sums(1)

    for cp in sent:
        cp.wait_send()

    @pl.loop(0, 2)
    def _(t):
        for q in range(3):
            for n in range(2):
                last_copy(t, q, n).wait_send()
                far_copy(t, q, n).wait_send()
            for n in range(4):
                pass_copy(t, q, n).wait_send()

        @pl.loop(0, 8)
        def _(i):
            sib_copy(t, i).wait_send()

    def sums_left(stage):
        @pl.loop(0, 2)
        def _(t):
            for q in range(3):
                for n in range(3):
                    if stage == 0 and q > 0:
                        half_copy(t, q, n, 0).wait_send()
                        half_copy(t, q, n, 1).wait_send()
                    else:
                        sum_copy(t, stage, q, n).wait_send()

    for stage in range(3):
        @pl.loop(0, 2)
        def _(t):
            for q in range(3):
                sum_end(t, stage, q)

        if stage < 2:
            sums_left(stage)

    for t in range(2):
        whole = fin[t, 0:2].reshape(64, 128)
        rolled = pltpu.roll(whole, 64, 1)
        f2 = fin[t, 2]
        r2 = pltpu.roll(f2, 64, 1)
        rows = slice(t * 64, (t + 1) * 64)
        mid[rows, 0:128] += jnp.where(
            odd, jnp.where(lane64, jnp.concatenate([r2, f2], axis=0), rolled), whole)
        mid[rows, 128:256] += jnp.where(odd, rolled, jnp.concatenate([f2, r2], axis=0))
    out_ref[0:128, :] = mid[:, 0:128].T.astype(bf16)
    out_ref[128:192, :] = mid[:, 128:256].T[0:64].astype(bf16)

    sums_left(2)


def shards(
    query,
    new_key,
    new_value,
    key_cache,
    value_cache,
    lengths,
    hidden_in,
    w_out,
    expert_ids,
    gate_weights,
    w_gate,
    w_up,
    w_down,
):
    bf16, f32 = jnp.bfloat16, jnp.float32
    hbm = pl.BlockSpec(memory_space=pl.ANY)
    mixed = pl.pallas_call(
        layer_kernel,
        out_shape=jax.ShapeDtypeStruct((192, 128), bf16),
        in_specs=[pl.BlockSpec(memory_space=pltpu.SMEM)] + [hbm] * 12,
        out_specs=pl.BlockSpec(memory_space=pltpu.VMEM),
        scratch_shapes=[
            pltpu.VMEM((4, 3072), bf16),
            pltpu.VMEM((4, 512), bf16),
            pltpu.VMEM((4, 512), bf16),
            pltpu.VMEM((2, 128), jnp.int32),
            pltpu.VMEM((2, 128), f32),
            pltpu.VMEM((192, 128), bf16),
            pltpu.VMEM((4, CONTEXT, 512), bf16),
            pltpu.VMEM((4, CONTEXT, 512), bf16),
            pltpu.VMEM((192, 3072), bf16),
            pltpu.VMEM((WIDTH, 4 * UNITS), bf16),
            pltpu.VMEM((2 * UNITS, WIDTH), bf16),
            pltpu.VMEM((96, 128), f32),
            pltpu.VMEM((96, 128), f32),
            pltpu.VMEM((2, 2, 4, 4, 48, 128), bf16),
            pltpu.VMEM((2, 3, 2, 4, 4, 4, 32, 128), bf16),
            pltpu.VMEM((2, 2, 8, 128), f32),
            pltpu.VMEM((2, 2, 256, 128), f32),
            pltpu.VMEM((2, 3, 2, 4, 4, 4, 32, 128), bf16),
            pltpu.VMEM((2, 3, 4, 4, 4, 32, 128), bf16),
            pltpu.VMEM((2, 3, 3, 4, 4, 32, 128), bf16),
            pltpu.VMEM((2, 3, 3, 4, 32, 128), bf16),
            pltpu.VMEM((2, 3, 3, 32, 128), bf16),
            pltpu.VMEM((256, 1024), f32),
            pltpu.VMEM((2, 256, 768), f32),
            pltpu.VMEM((256, 512), bf16),
            pltpu.VMEM((128, 256), f32),
            pltpu.VMEM((2, 3, 32, 128), f32),
            pltpu.SemaphoreType.DMA((26,)),
            pltpu.SemaphoreType.DMA((190,)),
            pltpu.SemaphoreType.DMA((190,)),
        ],
        compiler_params=pltpu.CompilerParams(
            collective_id=0, has_side_effects=True, vmem_limit_bytes=60 * 1024 * 1024
        ),
        cost_estimate=pl.CostEstimate(flops=10_000_000_000, bytes_accessed=25_000_000, transcendentals=0),
        name="layer",
    )(
        lengths, query, new_key, new_value, expert_ids.T, gate_weights.T, hidden_in.T,
        key_cache, value_cache, w_out.T, w_gate, w_up, w_down,
    )
    return mixed.T


def solution(mesh):
    return jax.shard_map(
        shards,
        mesh=mesh,
        in_specs=(
            P(("pool", "dev"), None),
            P(("pool", "dev"), None),
            P(("pool", "dev"), None),
            P(("pool", "dev"), None, None),
            P(("pool", "dev"), None, None),
            P(("pool", "dev")),
            P("pool", "dev"),
            P(None, "dev"),
            P("pool", None),
            P("pool", None),
            P("pool", None, "dev"),
            P("pool", None, "dev"),
            P("pool", "dev", None),
        ),
        out_specs=P("pool", "dev"),
        check_vma=False,
    )
```
